512 devices in a mesh: grp: 16 (over z), brick: 32 (over y, x, core).
Axes of the slice: x: 4, y: 4, z: 16, core: 2. Of those that a mesh axis runs over, the one named last changes fastest.
Arguments:
- probes: bfloat16 [65536, 256], P('brick'), may hold values from -6 to 6
- weights: bfloat16 [16, 256, 3, 256, 256], P('grp', 'brick'), may hold values from -0.21875 to 0.21875
- columns: int32 [16, 256, 3], P('grp', 'brick'), may hold values from 0 to 23, as said below
Outputs:
- basis: float32 [65536, 256], P('brick')
- triangle: float32 [256, 256], replicated
The draws below stay inside these ranges and needn't reach their ends.
Inputs may be any that keep to these rules, and one draw needn't show every extreme that they name: `columns`: for data block r the three ids are: 8 + r % 8, one id below 8, and one id of at least 16.
All inputs are finite; a program needn't handle non-finite values.
Results may differ from the reference program's by a relative error of at most 0.0029.
Values may be sent and summed in bfloat16 or wider, within the bound.
No kernel may reach another device: no remote copies, remote signals or barrier semaphores. Data moves between devices by JAX's collectives and lax.ppermute only.
A program may use at most 64 MiB of HBM per device.

```python
import math
import jax
import jax.numpy as jnp
from jax import lax

BS = 256
K = 256
NNZ = 3
NB = 8
NBLK = 256
NPARAM = 65536
N_GRP = 16
N_BRICK = 32


def draw_columns(key, part):
    key = jax.random.fold_in(key, 7)
    first_key, second_key = jax.random.split(key)
    rows = jnp.arange(N_GRP * NB * N_BRICK, dtype=jnp.int32).reshape(N_GRP, NB * N_BRICK)
    own = NB + rows % NB
    below = jax.random.randint(first_key, (N_GRP, NB * N_BRICK), 0, NB).astype(jnp.int32)
    above = jax.random.randint(second_key, (N_GRP, NB * N_BRICK), 2 * NB, 3 * NB).astype(jnp.int32)
    below = below.at[0, 0].set(0)
    above = above.at[0, NB * N_BRICK - 1].set(3 * NB - 1)
    return jnp.stack([own, below, above], axis=-1).astype(jnp.int32)


def block_scale(rng, shape, shards, smallest, top_value):
    loudness, own = 1.0, jax.random.fold_in(rng, 6)
    for position, shards_of in shards:
        draws = jnp.exp(jax.random.uniform(jax.random.fold_in(own, position), (shards_of,), jnp.float32, smallest / len(shards), top_value / len(shards)))
        loudness = loudness * jnp.repeat(draws, shape[position] // shards_of).reshape([-1 if axis == position else 1 for axis in range(len(shape))])
    return loudness


def scatter_about(stream_key, dims, deviation, bound, cuts=(), held_as=jnp.bfloat16):
    array = deviation * jax.random.normal(stream_key, dims, jnp.float32)
    if cuts:
        array = array * block_scale(stream_key, dims, cuts, -0.22, 0.18)
    return jnp.clip(array, -bound, bound).astype(held_as)


def setup_inputs(seed: int = 0) -> dict:
    arg_keys = jax.random.split(jax.random.key(seed), 4)
    probes = scatter_about(arg_keys[0], (NPARAM, K), 1.0, 6.0, ((0, 32),))
    weights = scatter_about(arg_keys[1], (N_GRP, NBLK, NNZ, BS, BS), (NNZ * BS) ** -0.5, 0.21875, ((0, 16), (1, 32)))
    columns = draw_columns(jax.random.fold_in(arg_keys[3], 71), 0)
    return dict(probes=probes, weights=weights, columns=columns)


def reference(probes, weights, columns):
    nblk = N_BRICK * NB
    blocks = probes.reshape(nblk, BS, K)
    rows = jnp.arange(nblk, dtype=jnp.int32)
    base = rows // NB * NB - NB

    def group_term(acc, pair):
        w_group, c_group = pair
        target = base[:, None] + c_group.astype(jnp.int32)
        valid = (target >= 0) & (target < nblk)
        safe = jnp.clip(target, 0, nblk - 1).astype(jnp.int32)
        picked = jnp.where(valid[:, :, None, None], blocks[safe], jnp.zeros((), blocks.dtype))
        w_float = w_group.astype(jnp.float32)
        data = jnp.einsum('rjac,rjck->rak', w_float, picked.astype(jnp.float32)).astype(jnp.bfloat16)
        contrib = jnp.einsum('rjac,rak->rjck', w_float, data.astype(jnp.float32))
        segment = jnp.where(valid, target, nblk).reshape(-1).astype(jnp.int32)
        summed = jax.ops.segment_sum(contrib.reshape(-1, BS, K), segment, num_segments=nblk + 1)[:nblk]
        return (acc + summed.reshape(nblk * BS, K), None)
    start = jnp.zeros((nblk * BS, K), jnp.float32)
    total, unused = lax.scan(group_term, start, (weights, columns))
    image = probes.astype(jnp.float32) + total
    gram = jnp.dot(image.T, image, precision=lax.Precision.HIGHEST)
    lower = jnp.linalg.cholesky(gram)
    basis = jax.scipy.linalg.solve_triangular(lower, image.T, lower=True).T
    factor = math.sqrt(nblk * BS)
    return (basis * factor, lower.T / factor)
```

```python
import functools
import math

import jax
import jax.numpy as jnp
from jax import lax
from jax.experimental import pallas as pl
from jax.experimental.pallas import tpu as pltpu
from jax.sharding import Mesh
from jax.sharding import PartitionSpec as P

F32 = jnp.float32
BF16 = jnp.bfloat16
PANEL = 64
MIB = 1024 * 1024
DEPTH = ("zh", "zp")


def exact_dot(a, b, dims):
    return lax.dot_general(
        a, b, (dims, ((), ())), precision=lax.Precision.HIGHEST, preferred_element_type=F32
    )


def split_dot(a, b, dims):
    a_high, b_high = a.astype(BF16), b.astype(BF16)
    a_low = (a - a_high.astype(F32)).astype(BF16)
    b_low = (b - b_high.astype(F32)).astype(BF16)
    dot = functools.partial(
        lax.dot_general, dimension_numbers=(dims, ((), ())), preferred_element_type=F32
    )
    return dot(a_high, b_high) + (dot(a_high, b_low) + dot(a_low, b_high))


def operator_kernel(cols, w_ref, low_ref, own_ref, high_ref, o_own, o_below, o_above, s_below, s_above):
    r = pl.program_id(0)
    half = own_ref.shape[0]

    @pl.when(r == 0)
    def _():
        s_below[...] = jnp.zeros_like(s_below)
        s_above[...] = jnp.zeros_like(s_above)

    ids = [cols[3 * r + j] for j in range(3)]
    at_low = jnp.where(ids[0] < half, 0, jnp.where(ids[1] < half, 1, 2))
    at_high = jnp.where(ids[0] >= 2 * half, 0, jnp.where(ids[1] >= 2 * half, 1, 2))
    at_own = 3 - at_low - at_high
    c_low = cols[3 * r + at_low]
    c_high = cols[3 * r + at_high] - 2 * half
    w_low, w_own, w_high = w_ref[0, at_low], w_ref[0, at_own], w_ref[0, at_high]
    data = (
        jnp.dot(w_low, low_ref[c_low], preferred_element_type=F32)
        + jnp.dot(w_own, own_ref[r], preferred_element_type=F32)
        + jnp.dot(w_high, high_ref[c_high], preferred_element_type=F32)
    ).astype(BF16)
    back = functools.partial(
        lax.dot_general, dimension_numbers=(((0,), (0,)), ((), ())), preferred_element_type=F32
    )
    o_own[0] = back(w_own, data)
    s_below[c_low] += back(w_low, data)
    s_above[c_high] += back(w_high, data)

    @pl.when(r == pl.num_programs(0) - 1)
    def _():
        o_below[...] = s_below[...].astype(BF16)
        o_above[...] = s_above[...].astype(BF16)


def apply_operator(cols, weights, low, own, high):
    blocks, slots, bs, _ = weights.shape
    width = own.shape[-1]
    whole = pl.BlockSpec((blocks, bs, width), lambda r, c: (0, 0, 0))
    shape = (blocks, bs, width)
    return pl.pallas_call(
        operator_kernel,
        grid_spec=pltpu.PrefetchScalarGridSpec(
            num_scalar_prefetch=1,
            grid=(blocks,),
            in_specs=[
                pl.BlockSpec((1, slots, bs, bs), lambda r, c: (r, 0, 0, 0)),
                whole,
                whole,
                whole,
            ],
            out_specs=[pl.BlockSpec((1, bs, width), lambda r, c: (r, 0, 0)), whole, whole],
            scratch_shapes=[pltpu.VMEM(shape, F32), pltpu.VMEM(shape, F32)],
        ),
        out_shape=(
            jax.ShapeDtypeStruct(shape, F32),
            jax.ShapeDtypeStruct(shape, BF16),
            jax.ShapeDtypeStruct(shape, BF16),
        ),
        compiler_params=pltpu.CompilerParams(vmem_limit_bytes=40 * MIB),
        name="normal_operator",
    )(cols, weights, low, own, high)


def halves_kernel(odd, *refs):
    ins, outs = refs[:12], refs[12:]
    for k in range(4):
        own, above, below = ins[3 * k : 3 * k + 3]
        total = own[0] + above[0].astype(F32) + below[0].astype(F32)
        outs[k][...] = total.astype(outs[k].dtype)


def split_halves(odd, own, above, below):
    rows, width = own.shape
    part, step = rows // 4, rows // 16
    arrays = [x.reshape(4, part, width) for x in (own, above, below)]
    places = (
        lambda s, o: (o[0], s, 0),
        lambda s, o: (1 - o[0], s, 0),
        lambda s, o: (2 + o[0], s, 0),
        lambda s, o: (3 - o[0], s, 0),
    )
    in_specs = [pl.BlockSpec((1, step, width), place) for place in places for _ in range(3)]
    out = pl.BlockSpec((step, width), lambda s, o: (s, 0))
    kept, sent = (jax.ShapeDtypeStruct((part, width), t) for t in (F32, BF16))
    return pl.pallas_call(
        halves_kernel,
        grid_spec=pltpu.PrefetchScalarGridSpec(
            num_scalar_prefetch=1, grid=(part // step,), in_specs=in_specs, out_specs=[out] * 4
        ),
        out_shape=(kept, sent, kept, sent),
        name="split_halves",
    )(odd, *(arrays * 4))


def pairs_kernel(ka, ra, kb, rb, out):
    n = ka.shape[0]
    out[:n] = (ka[...] + ra[...].astype(F32)).astype(BF16)
    out[n:] = (kb[...] + rb[...].astype(F32)).astype(BF16)


def add_pairs(ka, ra, kb, rb):
    rows, width = ka.shape
    return pl.pallas_call(
        pairs_kernel, out_shape=jax.ShapeDtypeStruct((2 * rows, width), BF16), name="add_pairs"
    )(ka, ra, kb, rb)


def image_kernel(block, pieces, probes, image, gram):
    total = probes[...].astype(F32)
    for k in range(pieces.shape[0]):
        total = total + pieces[k].astype(F32)
    image[...] = total
    gram[...] = exact_dot(total, total, ((0,), (0,)))


def image_and_gram(block, pieces, probes):
    count, rows, width = pieces.shape
    return pl.pallas_call(
        image_kernel,
        grid_spec=pltpu.PrefetchScalarGridSpec(
            num_scalar_prefetch=1,
            grid=(1,),
            in_specs=[
                pl.BlockSpec((count, rows, width), lambda i, b: (0, 0, 0)),
                pl.BlockSpec((rows, width), lambda i, b: (b[0], 0)),
            ],
            out_specs=[
                pl.BlockSpec((rows, width), lambda i, b: (0, 0)),
                pl.BlockSpec((width, width), lambda i, b: (0, 0)),
            ],
        ),
        out_shape=(
            jax.ShapeDtypeStruct((rows, width), F32),
            jax.ShapeDtypeStruct((width, width), F32),
        ),
        name="image_and_gram",
    )(block, pieces, probes)


def spread_sum_kernel(pieces, out):
    total = pieces[0]
    for k in range(1, pieces.shape[0]):
        total = total + pieces[k]
    for k in range(out.shape[0]):
        out[k] = total


def spread_sum(pieces, copies):
    return pl.pallas_call(
        spread_sum_kernel,
        out_shape=jax.ShapeDtypeStruct((copies,) + pieces.shape[1:], F32),
        name="spread_sum",
    )(pieces)


def eliminate(tiles, lane0):
    count, wide = len(tiles), len(tiles[0])
    sub = lax.broadcasted_iota(jnp.int32, (8, 128), 0)
    out = []
    for j in range(count):
        head = tiles[j]

        def columns(tile):
            first = lane0 + 8 * j
            return [
                jnp.broadcast_to(tile[0][:, first + k : first + k + 1], (8, 128)) for k in range(8)
            ]

        cols = columns(head)
        s = [[jnp.broadcast_to(cols[k][i : i + 1, :], (8, 128)) for k in range(i + 1)] for i in range(8)]
        low = [[None] * 8 for _ in range(8)]
        inv = [None] * 8
        for k in range(8):
            inv[k] = lax.rsqrt(s[k][k])
            for i in range(k + 1, 8):
                low[i][k] = s[i][k] * inv[k]
            for i in range(k + 1, 8):
                for m in range(k + 1, i + 1):
                    s[i][m] = s[i][m] - low[i][k] * low[m][k]
        u = []
        for i in range(8):
            parts = []
            for v in range(wide):
                a = jnp.broadcast_to(head[v][i : i + 1, :], (8, 128))
                for k in range(i):
                    a = a - low[i][k] * u[k][v]
                parts.append(a * inv[i])
            u.append(parts)
        rows = []
        for v in range(wide):
            t = u[0][v]
            for i in range(1, 8):
                t = jnp.where(sub == i, u[i][v], t)
            rows.append(t)
        out.append(rows)
        for r in range(j + 1, count):
            c = columns(tiles[r])
            l = []
            for i in range(8):
                a = c[i]
                for k in range(i):
                    a = a - low[i][k] * l[k]
                l.append(a * inv[i])
            new = []
            for v in range(wide):
                t = tiles[r][v]
                for i in range(8):
                    t = t - l[i] * u[i][v]
                new.append(t)
            tiles[r] = new
    return out


def factor_kernel(scale, gram, upper, inverse, work):
    n = gram.shape[0]
    panels = n // PANEL
    lane = lax.broadcasted_iota(jnp.int32, (8, 128), 1)
    sub = lax.broadcasted_iota(jnp.int32, (8, 128), 0)
    src = gram
    for p in range(panels):
        r0 = p * PANEL
        first, lane0 = r0 // 128, r0 % 128
        used = range(first, n // 128)
        tiles = []
        for t in range(PANEL // 8):
            row = src[r0 + 8 * t : r0 + 8 * t + 8, :]
            unit = jnp.where(lane == sub + 8 * t, 1.0, 0.0).astype(F32)
            tiles.append([row[:, 128 * v : 128 * v + 128] for v in used] + [unit])
        out = eliminate(tiles, lane0)
        rows = [jnp.concatenate([o[v] for o in out], axis=0) for v in range(len(used))]
        corner = jnp.concatenate([o[-1] for o in out], axis=0)[:, :PANEL]
        rows = [jnp.zeros((PANEL, 128), F32)] * first + rows
        u = jnp.concatenate(rows, axis=1)
        row_id = lax.broadcasted_iota(jnp.int32, (PANEL, n), 0) + r0
        col_id = lax.broadcasted_iota(jnp.int32, (PANEL, n), 1)
        u = jnp.where(col_id >= row_id, u, 0.0)
        work[r0 : r0 + PANEL, :] = u
        upper[r0 : r0 + PANEL, :] = u * (1.0 / scale)
        for q0 in range(r0 + PANEL, n, PANEL):
            update = exact_dot(u[:, q0 : q0 + PANEL], u, ((0,), (0,)))
            work[q0 : q0 + PANEL, :] = src[q0 : q0 + PANEL, :] - update
        src = work
        right = jnp.where(col_id == row_id, 1.0, 0.0).astype(F32)
        if p:
            right = right - exact_dot(work[0:r0, r0 : r0 + PANEL], inverse[0:r0, :], ((0,), (0,)))
        inverse[r0 : r0 + PANEL, :] = exact_dot(corner, right, ((1,), (0,)))


def cholesky_and_inverse(gram, scale):
    n = gram.shape[0]
    shape = jax.ShapeDtypeStruct((n, n), F32)
    return pl.pallas_call(
        functools.partial(factor_kernel, scale),
        out_shape=(shape, shape),
        scratch_shapes=[pltpu.VMEM((n, n), F32)],
        compiler_params=pltpu.CompilerParams(vmem_limit_bytes=16 * MIB),
        name="cholesky_and_inverse",
    )(gram)


def basis_kernel(scale, image, inverse, out):
    x = image[0, :, 0].reshape(out.shape)
    out[...] = split_dot(x, inverse[...] * scale, ((1,), (1,)))


def make_basis(image, inverse, scale):
    rows, width = image.shape[-2:]
    view = image.reshape(2, 4, 2, rows, width)
    return pl.pallas_call(
        functools.partial(basis_kernel, scale),
        grid=(2, 2),
        in_specs=[
            pl.BlockSpec((1, 4, 1, rows, width), lambda h, o: (h, 0, o, 0, 0)),
            pl.BlockSpec((width, width), lambda h, o: (0, 0)),
        ],
        out_specs=pl.BlockSpec((4 * rows, width), lambda h, o: (2 * h + o, 0)),
        out_shape=jax.ShapeDtypeStruct((16 * rows, width), F32),
        name="make_basis",
    )(view, inverse)


def shifted(value, axis, steps):
    count = lax.axis_size(axis)
    leading, last = (max(0, -steps), min(count, count - steps))
    return lax.ppermute(value, axis, [(source, source + steps) for source in range(leading, last)])


def body(probes, weights, columns):
    rows, width = probes.shape
    w_local = weights[0]
    blocks, _, bs, _ = w_local.shape
    low = shifted(probes, "brick", 1)
    high = shifted(probes, "brick", -1)
    shape = (blocks, bs, width)
    own, below, above = apply_operator(
        columns.reshape(-1), w_local, low.reshape(shape), probes.reshape(shape), high.reshape(shape)
    )
    from_above = shifted(below.reshape(rows, width), "brick", -1)
    from_below = shifted(above.reshape(rows, width), "brick", 1)

    zh, zp = lax.axis_index("zh"), lax.axis_index("zp")
    odd = jnp.full((1,), zp, jnp.int32)
    keep_a, send_a, keep_b, send_b = split_halves(odd, own.reshape(rows, width), from_above, from_below)
    n = lax.axis_size("zh") * lax.axis_size("zp")
    got_a = lax.ppermute(send_a, DEPTH, [(i, i ^ 1) for i in range(n)])
    got_b = lax.ppermute(send_b, DEPTH, [(i, (((i + 1) ^ 1) - 1) % n) for i in range(n)])
    held = add_pairs(keep_a, got_a, keep_b, got_b)
    pieces = lax.all_to_all(held.reshape(n // 2, rows // n, width), "zh", 0, 0)
    block = (zh // 4) * 8 + zp * 4 + zh % 4
    image, gram = image_and_gram(jnp.full((1,), block, jnp.int32), pieces, probes)
    whole_image = lax.all_gather(image, DEPTH)

    bricks = lax.axis_size("brick")
    share = lax.all_to_all(gram.reshape(bricks, width // bricks, width), "brick", 0, 0)
    share = lax.all_to_all(spread_sum(share, n), DEPTH, 0, 0)
    gram = lax.all_to_all(spread_sum(share, bricks), "brick", 0, 0).reshape(width, width)

    scale = math.sqrt(rows * bricks)
    upper, inverse = cholesky_and_inverse(gram, scale)
    return make_basis(whole_image, inverse, scale), upper


def solution(mesh):
    deep = mesh.devices.reshape(mesh.devices.shape[0] // 2, 2, mesh.devices.shape[1])
    mesh = Mesh(deep, DEPTH + ("brick",))
    in_specs = (P("brick", None), P(DEPTH, "brick", None, None, None), P(DEPTH, "brick", None))
    out_specs = (P("brick", None), P())
    return jax.shard_map(body, mesh=mesh, in_specs=in_specs, out_specs=out_specs, check_vma=False)
```

```python
import functools
import math

import jax
import jax.numpy as jnp
from jax import lax
from jax.experimental import pallas as pl
from jax.experimental.pallas import tpu as pltpu
from jax.sharding import Mesh
from jax.sharding import PartitionSpec as P

F32 = jnp.float32
BF16 = jnp.bfloat16
PANEL = 64
MIB = 1024 * 1024
DEPTH = ("zh", "zp")


def exact_dot(a, b, dims):
    return lax.dot_general(
        a, b, (dims, ((), ())), precision=lax.Precision.HIGHEST, preferred_element_type=F32
    )


def in_vmem():
    return pl.BlockSpec(memory_space=pltpu.VMEM)


def params(mib):
    return pltpu.CompilerParams(vmem_limit_bytes=mib * MIB)


def operator_kernel(cols, w_hbm, low_ref, own_ref, high_ref, o_own, o_below, o_above, w_ref, s_below, s_above, sems):
    blocks = own_ref.shape[0]

    def fetch(r):
        return pltpu.make_async_copy(w_hbm.at[r], w_ref.at[r], sems.at[r])

    for r in range(blocks):
        fetch(r).start()
    s_below[...] = jnp.zeros_like(s_below)
    s_above[...] = jnp.zeros_like(s_above)

    def step(r, carry):
        ids = [cols[3 * r + j] for j in range(3)]
        at_low = jnp.where(ids[0] < blocks, 0, jnp.where(ids[1] < blocks, 1, 2))
        at_high = jnp.where(ids[0] >= 2 * blocks, 0, jnp.where(ids[1] >= 2 * blocks, 1, 2))
        at_own = 3 - at_low - at_high
        c_low = cols[3 * r + at_low]
        c_high = cols[3 * r + at_high] - 2 * blocks
        fetch(r).wait()
        w_low, w_own, w_high = w_ref[r, at_low], w_ref[r, at_own], w_ref[r, at_high]
        dot = functools.partial(jnp.dot, preferred_element_type=F32)
        data = dot(w_low, low_ref[c_low]) + dot(w_own, own_ref[r]) + dot(w_high, high_ref[c_high])
        data = data.T.astype(BF16)
        term = dot(data, w_own)
        o_own[2 * r] = term[:, :128]
        o_own[2 * r + 1] = term[:, 128:]
        s_below[c_low] += dot(data, w_low)
        s_above[c_high] += dot(data, w_high)
        return carry

    lax.fori_loop(0, blocks, step, 0)
    for q in range(blocks):
        for field, out in ((s_below, o_below), (s_above, o_above)):
            out[2 * q] = field[q, :, :128].astype(BF16)
            out[2 * q + 1] = field[q, :, 128:].astype(BF16)


def apply_operator(cols, weights, low, own, high):
    blocks, slots, bs, _ = weights.shape
    width = own.shape[-1]
    shape = (2 * blocks, width, bs // 2)
    field = pltpu.VMEM((blocks, width, bs), F32)
    return pl.pallas_call(
        operator_kernel,
        in_specs=[
            pl.BlockSpec(memory_space=pltpu.SMEM),
            pl.BlockSpec(memory_space=pltpu.HBM),
            in_vmem(),
            in_vmem(),
            in_vmem(),
        ],
        out_specs=[in_vmem()] * 3,
        out_shape=(
            jax.ShapeDtypeStruct(shape, F32),
            jax.ShapeDtypeStruct(shape, BF16),
            jax.ShapeDtypeStruct(shape, BF16),
        ),
        scratch_shapes=[
            pltpu.VMEM(weights.shape, BF16),
            field,
            field,
            pltpu.SemaphoreType.DMA((blocks,)),
        ],
        compiler_params=params(24),
        name="normal_operator",
    )(cols, weights, low, own, high)


def halves_kernel(odd, own, above, below, keep_a, send_a, keep_b, send_b):
    part = keep_a.shape[0]
    o = odd[0]
    for out, first in ((keep_a, o), (send_a, 1 - o), (keep_b, 2 + o), (send_b, 3 - o)):
        for i in range(part):
            p = part * first + i
            out[i] = (own[p] + (above[p].astype(F32) + below[p].astype(F32))).astype(out.dtype)


def split_halves(odd, own, above, below):
    pieces, width, cells = own.shape
    kept, sent = (jax.ShapeDtypeStruct((pieces // 4, width, cells), t) for t in (F32, BF16))
    return pl.pallas_call(
        halves_kernel,
        in_specs=[pl.BlockSpec(memory_space=pltpu.SMEM)] + [in_vmem()] * 3,
        out_specs=[in_vmem()] * 4,
        out_shape=(kept, sent, kept, sent),
        compiler_params=params(12),
        name="split_halves",
    )(odd, own, above, below)


def pairs_kernel(ka, ra, kb, rb, out):
    n = ka.shape[0]
    for i in range(n):
        out[i] = (ka[i] + ra[i].astype(F32)).astype(BF16)
        out[n + i] = (kb[i] + rb[i].astype(F32)).astype(BF16)


def add_pairs(ka, ra, kb, rb):
    n, width, cells = ka.shape
    return pl.pallas_call(
        pairs_kernel,
        in_specs=[in_vmem()] * 4,
        out_specs=in_vmem(),
        out_shape=jax.ShapeDtypeStruct((2 * n, width, cells), BF16),
        compiler_params=params(8),
        name="add_pairs",
    )(ka, ra, kb, rb)


def image_kernel(block, pieces, probes, image, own, sem):
    rows = own.shape[0]
    copy = pltpu.make_async_copy(probes.at[pl.ds(block[0] * rows, rows)], own, sem)
    copy.start()
    total = pieces[0].astype(F32)
    for k in range(1, pieces.shape[0]):
        total = total + pieces[k].astype(F32)
    copy.wait()
    image[...] = own[...].astype(F32) + total.T


def make_image(block, pieces, probes):
    _, width, cells = pieces.shape
    return pl.pallas_call(
        image_kernel,
        in_specs=[
            pl.BlockSpec(memory_space=pltpu.SMEM),
            in_vmem(),
            pl.BlockSpec(memory_space=pltpu.HBM),
        ],
        out_specs=in_vmem(),
        out_shape=jax.ShapeDtypeStruct((cells, width), F32),
        scratch_shapes=[pltpu.VMEM((cells, width), BF16), pltpu.SemaphoreType.DMA],
        compiler_params=params(4),
        name="make_image",
    )(block, pieces, probes)


def gram_kernel(image, gram):
    gram[...] = exact_dot(image[...], image[...], ((0,), (0,)))


def make_gram(image):
    width = image.shape[1]
    return pl.pallas_call(
        gram_kernel,
        in_specs=[in_vmem()],
        out_specs=in_vmem(),
        out_shape=jax.ShapeDtypeStruct((width, width), F32),
        compiler_params=params(8),
        name="make_gram",
    )(image)


def spread_sum_kernel(pieces, out):
    total = pieces[0]
    for k in range(1, pieces.shape[0]):
        total = total + pieces[k]
    for k in range(out.shape[0]):
        out[k] = total


def spread_sum(pieces, copies):
    return pl.pallas_call(
        spread_sum_kernel,
        in_specs=[in_vmem()],
        out_specs=in_vmem(),
        out_shape=jax.ShapeDtypeStruct((copies,) + pieces.shape[1:], F32),
        compiler_params=params(4),
        name="spread_sum",
    )(pieces)


def eliminate(tiles, lane0):
    count, wide = len(tiles), len(tiles[0])
    sub = lax.broadcasted_iota(jnp.int32, (8, 128), 0)
    out = []
    for j in range(count):
        head = tiles[j]

        def columns(tile):
            first = lane0 + 8 * j
            return [
                jnp.broadcast_to(tile[0][:, first + k : first + k + 1], (8, 128)) for k in range(8)
            ]

        cols = columns(head)
        s = [[jnp.broadcast_to(cols[k][i : i + 1, :], (8, 128)) for k in range(i + 1)] for i in range(8)]
        low = [[None] * 8 for _ in range(8)]
        inv = [None] * 8
        for k in range(8):
            inv[k] = lax.rsqrt(s[k][k])
            for i in range(k + 1, 8):
                low[i][k] = s[i][k] * inv[k]
            for i in range(k + 1, 8):
                for m in range(k + 1, i + 1):
                    s[i][m] = s[i][m] - low[i][k] * low[m][k]
        u = []
        for i in range(8):
            parts = []
            for v in range(wide):
                a = jnp.broadcast_to(head[v][i : i + 1, :], (8, 128))
                for k in range(i):
                    a = a - low[i][k] * u[k][v]
                parts.append(a * inv[i])
            u.append(parts)
        rows = []
        for v in range(wide):
            t = u[0][v]
            for i in range(1, 8):
                t = jnp.where(sub == i, u[i][v], t)
            rows.append(t)
        out.append(rows)
        for r in range(j + 1, count):
            c = columns(tiles[r])
            l = []
            for i in range(8):
                a = c[i]
                for k in range(i):
                    a = a - low[i][k] * l[k]
                l.append(a * inv[i])
            new = []
            for v in range(wide):
                t = tiles[r][v]
                for i in range(8):
                    t = t - l[i] * u[i][v]
                new.append(t)
            tiles[r] = new
    return out


def factor_kernel(scale, gram, upper, high, low, work, inverse):
    n = gram.shape[0]
    panels = n // PANEL
    lane = lax.broadcasted_iota(jnp.int32, (8, 128), 1)
    sub = lax.broadcasted_iota(jnp.int32, (8, 128), 0)
    src = gram
    for p in range(panels):
        r0 = p * PANEL
        first, lane0 = r0 // 128, r0 % 128
        used = range(first, n // 128)
        tiles = []
        for t in range(PANEL // 8):
            row = src[r0 + 8 * t : r0 + 8 * t + 8, :]
            unit = jnp.where(lane == sub + 8 * t, 1.0, 0.0).astype(F32)
            tiles.append([row[:, 128 * v : 128 * v + 128] for v in used] + [unit])
        out = eliminate(tiles, lane0)
        rows = [jnp.concatenate([o[v] for o in out], axis=0) for v in range(len(used))]
        corner = jnp.concatenate([o[-1] for o in out], axis=0)[:, :PANEL]
        rows = [jnp.zeros((PANEL, 128), F32)] * first + rows
        u = jnp.concatenate(rows, axis=1)
        row_id = lax.broadcasted_iota(jnp.int32, (PANEL, n), 0) + r0
        col_id = lax.broadcasted_iota(jnp.int32, (PANEL, n), 1)
        u = jnp.where(col_id >= row_id, u, 0.0)
        work[r0 : r0 + PANEL, :] = u
        upper[r0 : r0 + PANEL, :] = u * (1.0 / scale)
        for q0 in range(r0 + PANEL, n, PANEL):
            update = exact_dot(u[:, q0 : q0 + PANEL], u, ((0,), (0,)))
            work[q0 : q0 + PANEL, :] = src[q0 : q0 + PANEL, :] - update
        src = work
        right = jnp.where(col_id == row_id, 1.0, 0.0).astype(F32)
        if p:
            right = right - exact_dot(work[0:r0, r0 : r0 + PANEL], inverse[0:r0, :], ((0,), (0,)))
        inverse[r0 : r0 + PANEL, :] = exact_dot(corner, right, ((1,), (0,)))
    turned = inverse[...].T * scale
    high[...] = turned.astype(BF16)
    low[...] = (turned - high[...].astype(F32)).astype(BF16)


def cholesky_and_inverse(gram, scale):
    n = gram.shape[0]
    full, half = (jax.ShapeDtypeStruct((n, n), t) for t in (F32, BF16))
    return pl.pallas_call(
        functools.partial(factor_kernel, scale),
        in_specs=[in_vmem()],
        out_specs=[in_vmem()] * 3,
        out_shape=(full, half, half),
        scratch_shapes=[pltpu.VMEM((n, n), F32)] * 2,
        compiler_params=params(8),
        name="cholesky_and_inverse",
    )(gram)


def basis_kernel(image, high, low, out):
    x = image[0, :, 0].reshape(out.shape)
    x_high = x.astype(BF16)
    x_low = (x - x_high.astype(F32)).astype(BF16)
    dot = functools.partial(jnp.dot, preferred_element_type=F32)
    out[...] = dot(x_high, high[...]) + (dot(x_high, low[...]) + dot(x_low, high[...]))


def make_basis(image, high, low):
    rows, width = image.shape[-2:]
    view = image.reshape(2, 4, 2, rows, width)
    return pl.pallas_call(
        basis_kernel,
        grid=(2, 2),
        in_specs=[
            pl.BlockSpec((1, 4, 1, rows, width), lambda h, o: (h, 0, o, 0, 0)),
            in_vmem(),
            in_vmem(),
        ],
        out_specs=pl.BlockSpec((4 * rows, width), lambda h, o: (2 * h + o, 0)),
        out_shape=jax.ShapeDtypeStruct((16 * rows, width), F32),
        compiler_params=params(16),
        name="make_basis",
    )(view, high, low)


def shifted(value, axis, steps):
    count = lax.axis_size(axis)
    leading, last = (max(0, -steps), min(count, count - steps))
    return lax.ppermute(value, axis, [(source, source + steps) for source in range(leading, last)])


def body(probes, weights, columns):
    rows, width = probes.shape
    w_local = weights[0]
    blocks, _, bs, _ = w_local.shape
    lower = shifted(probes, "brick", 1)
    higher = shifted(probes, "brick", -1)
    shape = (blocks, bs, width)
    own, below, above = apply_operator(
        columns.reshape(-1), w_local, lower.reshape(shape), probes.reshape(shape), higher.reshape(shape)
    )
    from_above = shifted(below, "brick", -1)
    from_below = shifted(above, "brick", 1)

    zh, zp = lax.axis_index("zh"), lax.axis_index("zp")
    odd = jnp.full((1,), zp, jnp.int32)
    keep_a, send_a, keep_b, send_b = split_halves(odd, own, from_above, from_below)
    n = lax.axis_size("zh") * lax.axis_size("zp")
    got_a = lax.ppermute(send_a, DEPTH, [(i, i ^ 1) for i in range(n)])
    got_b = lax.ppermute(send_b, DEPTH, [(i, (((i + 1) ^ 1) - 1) % n) for i in range(n)])
    pieces = lax.all_to_all(add_pairs(keep_a, got_a, keep_b, got_b), "zh", 0, 0)
    block = (zh // 4) * 8 + zp * 4 + zh % 4
    image = make_image(jnp.full((1,), block, jnp.int32), pieces, probes)
    whole_image = lax.all_gather(image, DEPTH)
    gram = make_gram(image)

    bricks = lax.axis_size("brick")
    share = lax.all_to_all(gram.reshape(bricks, width // bricks, width), "brick", 0, 0)
    share = lax.all_to_all(spread_sum(share, n), DEPTH, 0, 0)
    gram = lax.all_to_all(spread_sum(share, bricks), "brick", 0, 0).reshape(width, width)

    scale = math.sqrt(rows * bricks)
    upper, high, low = cholesky_and_inverse(gram, scale)
    return make_basis(whole_image, high, low), upper


def solution(mesh):
    deep = mesh.devices.reshape(mesh.devices.shape[0] // 2, 2, mesh.devices.shape[1])
    mesh = Mesh(deep, DEPTH + ("brick",))
    in_specs = (P("brick", None), P(DEPTH, "brick", None, None, None), P(DEPTH, "brick", None))
    out_specs = (P("brick", None), P())
    return jax.shard_map(body, mesh=mesh, in_specs=in_specs, out_specs=out_specs, check_vma=False)
```

```python
import functools
import math

import jax
import jax.numpy as jnp
from jax import lax
from jax.experimental import pallas as pl
from jax.experimental.pallas import tpu as pltpu
from jax.sharding import Mesh
from jax.sharding import PartitionSpec as P

F32 = jnp.float32
BF16 = jnp.bfloat16
PANEL = 64
MIB = 1024 * 1024
AHEAD = 4
DEPTH = ("zh", "zp")


def exact_dot(a, b, dims):
    return lax.dot_general(
        a, b, (dims, ((), ())), precision=lax.Precision.HIGHEST, preferred_element_type=F32
    )


def in_vmem():
    return pl.BlockSpec(memory_space=pltpu.VMEM)


def params(mib):
    return pltpu.CompilerParams(vmem_limit_bytes=mib * MIB)


def operator_kernel(
    cols, odd, w_hbm, far_hbm, own_hbm, near_hbm, own_out, far_out, near_out,
    w_ref, p_ref, s_own, s_far, s_near, h_far, h_near, d_ref, in_sems, out_sems,
):
    blocks = p_ref.shape[0]
    dot = functools.partial(jnp.dot, preferred_element_type=F32)

    def places(r):
        ids = [cols[3 * r + j] for j in range(3)]
        at_low = jnp.where(ids[0] < blocks, 0, jnp.where(ids[1] < blocks, 1, 2))
        at_high = jnp.where(ids[0] >= 2 * blocks, 0, jnp.where(ids[1] >= 2 * blocks, 1, 2))
        at_own = 3 - at_low - at_high
        low, high = cols[3 * r + at_low], cols[3 * r + at_high] - 2 * blocks
        first = odd[0] == 0
        at = (jnp.where(first, at_low, at_high), at_own, jnp.where(first, at_high, at_low))
        return at, jnp.where(first, low, high), jnp.where(first, high, low)

    def fetch(r):
        at, far, near = places(r)
        sources = ((far_hbm, far), (own_hbm, r), (near_hbm, near))
        return [
            pltpu.make_async_copy(w_hbm.at[r, at[j]], w_ref.at[r, j], in_sems.at[r, j])
            for j in range(3)
        ] + [
            pltpu.make_async_copy(source.at[q], p_ref.at[r, j], in_sems.at[r, 3 + j])
            for j, (source, q) in enumerate(sources)
        ]

    def weights_of(r):
        return jnp.concatenate([w_ref[r, j] for j in range(3)], axis=1)

    def data_of(r):
        probes = jnp.concatenate([p_ref[r, j] for j in range(3)], axis=0)
        return dot(weights_of(r), probes).astype(BF16).T

    def own_copy(r):
        return pltpu.make_async_copy(s_own.at[r], own_out.at[r], out_sems.at[r])

    def put(r, terms):
        _, far, near = places(r)
        bs = terms.shape[1] // 3
        s_own[r, 0] = terms[:, bs : bs + 128]
        s_own[r, 1] = terms[:, bs + 128 : 2 * bs]
        own_copy(r).start()
        s_far[far] += terms[:, :bs]
        s_near[near] += terms[:, 2 * bs :]

    for r in range(AHEAD):
        for copy in fetch(r):
            copy.start()
    s_far[...] = jnp.zeros_like(s_far)
    s_near[...] = jnp.zeros_like(s_near)
    for copy in fetch(0):
        copy.wait()
    d_ref[0] = data_of(0)

    def step(r, carry):
        @pl.when(r + AHEAD < blocks)
        def _():
            for copy in fetch(r + AHEAD):
                copy.start()

        for copy in fetch(r + 1):
            copy.wait()
        terms = dot(d_ref[r % 2], weights_of(r))
        d_ref[(r + 1) % 2] = data_of(r + 1)
        put(r, terms)
        return carry

    lax.fori_loop(0, blocks - 1, step, 0)
    put(blocks - 1, dot(d_ref[(blocks - 1) % 2], weights_of(blocks - 1)))
    last = []
    for k, (field, half, out) in enumerate(((s_far, h_far, far_out), (s_near, h_near, near_out))):
        for q in range(blocks):
            half[2 * q] = field[q, :, :128].astype(BF16)
            half[2 * q + 1] = field[q, :, 128:].astype(BF16)
            pair = pl.ds(2 * q, 2)
            copy = pltpu.make_async_copy(half.at[pair], out.at[pair], out_sems.at[(k + 1) * blocks + q])
            copy.start()
            last.append(copy)
    for r in range(blocks):
        own_copy(r).wait()
    for copy in last:
        copy.wait()


def apply_operator(cols, odd, weights, far, own, near):
    blocks, slots, bs, _ = weights.shape
    width = own.shape[-1]
    shape = (2 * blocks, width, bs // 2)
    smem, hbm = pl.BlockSpec(memory_space=pltpu.SMEM), pl.BlockSpec(memory_space=pl.ANY)
    field = pltpu.VMEM((blocks, width, bs), F32)
    half = pltpu.VMEM(shape, BF16)
    own_field, far_field, near_field = pl.pallas_call(
        operator_kernel,
        in_specs=[smem, smem] + [hbm] * 4,
        out_specs=[hbm] * 3,
        out_shape=(
            jax.ShapeDtypeStruct((blocks, 2, width, bs // 2), F32),
            jax.ShapeDtypeStruct(shape, BF16),
            jax.ShapeDtypeStruct(shape, BF16),
        ),
        scratch_shapes=[
            pltpu.VMEM(weights.shape, BF16),
            pltpu.VMEM((blocks, 3, bs, width), BF16),
            pltpu.VMEM((blocks, 2, width, bs // 2), F32),
            field,
            field,
            half,
            half,
            pltpu.VMEM((2, width, bs), BF16),
            pltpu.SemaphoreType.DMA((blocks, 6)),
            pltpu.SemaphoreType.DMA((3 * blocks,)),
        ],
        compiler_params=params(60),
        name="normal_operator",
    )(cols, odd, weights, far, own, near)
    return own_field.reshape(shape), far_field, near_field


def halves_kernel(odd, own, far, near, keep_a, send_a, keep_b, send_b):
    part = keep_a.shape[0]
    o = odd[0]
    for out, first in ((keep_a, o), (send_a, 1 - o), (keep_b, 2 + o), (send_b, 3 - o)):
        for i in range(part):
            p = part * first + i
            out[i] = (own[p] + (far[p].astype(F32) + near[p].astype(F32))).astype(out.dtype)


def split_halves(odd, own, far, near):
    pieces, width, cells = own.shape
    kept, sent = (jax.ShapeDtypeStruct((pieces // 4, width, cells), t) for t in (F32, BF16))
    return pl.pallas_call(
        halves_kernel,
        in_specs=[pl.BlockSpec(memory_space=pltpu.SMEM)] + [in_vmem()] * 3,
        out_specs=[in_vmem()] * 4,
        out_shape=(kept, sent, kept, sent),
        compiler_params=params(12),
        name="split_halves",
    )(odd, own, far, near)


def pairs_kernel(ka, ra, kb, rb, out):
    n = ka.shape[0]
    for i in range(n):
        out[i] = (ka[i] + ra[i].astype(F32)).astype(BF16)
        out[n + i] = (kb[i] + rb[i].astype(F32)).astype(BF16)


def add_pairs(ka, ra, kb, rb):
    n, width, cells = ka.shape
    return pl.pallas_call(
        pairs_kernel,
        in_specs=[in_vmem()] * 4,
        out_specs=in_vmem(),
        out_shape=jax.ShapeDtypeStruct((2 * n, width, cells), BF16),
        compiler_params=params(8),
        name="add_pairs",
    )(ka, ra, kb, rb)


def image_kernel(block, pieces, probes, image, own, sem):
    rows = own.shape[0]
    copy = pltpu.make_async_copy(probes.at[pl.ds(block[0] * rows, rows)], own, sem)
    copy.start()
    total = pieces[0].astype(F32)
    for k in range(1, pieces.shape[0]):
        total = total + pieces[k].astype(F32)
    copy.wait()
    image[...] = own[...].astype(F32) + total.T


def make_image(block, pieces, probes):
    _, width, cells = pieces.shape
    return pl.pallas_call(
        image_kernel,
        in_specs=[
            pl.BlockSpec(memory_space=pltpu.SMEM),
            in_vmem(),
            pl.BlockSpec(memory_space=pltpu.HBM),
        ],
        out_specs=in_vmem(),
        out_shape=jax.ShapeDtypeStruct((cells, width), F32),
        scratch_shapes=[pltpu.VMEM((cells, width), BF16), pltpu.SemaphoreType.DMA],
        compiler_params=params(4),
        name="make_image",
    )(block, pieces, probes)


def gram_kernel(image, gram):
    gram[...] = exact_dot(image[...], image[...], ((0,), (0,)))


def make_gram(image):
    width = image.shape[1]
    return pl.pallas_call(
        gram_kernel,
        in_specs=[in_vmem()],
        out_specs=in_vmem(),
        out_shape=jax.ShapeDtypeStruct((width, width), F32),
        compiler_params=params(8),
        name="make_gram",
    )(image)


def spread_sum_kernel(pieces, out):
    total = pieces[0]
    for k in range(1, pieces.shape[0]):
        total = total + pieces[k]
    for k in range(out.shape[0]):
        out[k] = total


def spread_sum(pieces, copies):
    return pl.pallas_call(
        spread_sum_kernel,
        in_specs=[in_vmem()],
        out_specs=in_vmem(),
        out_shape=jax.ShapeDtypeStruct((copies,) + pieces.shape[1:], F32),
        compiler_params=params(4),
        name="spread_sum",
    )(pieces)


def eliminate(tiles, lane0):
    count, wide = len(tiles), len(tiles[0])
    sub = lax.broadcasted_iota(jnp.int32, (8, 128), 0)
    out = []
    for j in range(count):
        head = tiles[j]

        def columns(tile):
            first = lane0 + 8 * j
            return [
                jnp.broadcast_to(tile[0][:, first + k : first + k + 1], (8, 128)) for k in range(8)
            ]

        cols = columns(head)
        s = [[jnp.broadcast_to(cols[k][i : i + 1, :], (8, 128)) for k in range(i + 1)] for i in range(8)]
        low = [[None] * 8 for _ in range(8)]
        inv = [None] * 8
        for k in range(8):
            inv[k] = lax.rsqrt(s[k][k])
            for i in range(k + 1, 8):
                low[i][k] = s[i][k] * inv[k]
            for i in range(k + 1, 8):
                for m in range(k + 1, i + 1):
                    s[i][m] = s[i][m] - low[i][k] * low[m][k]
        u = []
        for i in range(8):
            parts = []
            for v in range(wide):
                a = jnp.broadcast_to(head[v][i : i + 1, :], (8, 128))
                for k in range(i):
                    a = a - low[i][k] * u[k][v]
                parts.append(a * inv[i])
            u.append(parts)
        rows = []
        for v in range(wide):
            t = u[0][v]
            for i in range(1, 8):
                t = jnp.where(sub == i, u[i][v], t)
            rows.append(t)
        out.append(rows)
        for r in range(j + 1, count):
            c = columns(tiles[r])
            l = []
            for i in range(8):
                a = c[i]
                for k in range(i):
                    a = a - low[i][k] * l[k]
                l.append(a * inv[i])
            new = []
            for v in range(wide):
                t = tiles[r][v]
                for i in range(8):
                    t = t - l[i] * u[i][v]
                new.append(t)
            tiles[r] = new
    return out


def factor_kernel(scale, gram, upper, high, low, work, inverse):
    n = gram.shape[0]
    panels = n // PANEL
    lane = lax.broadcasted_iota(jnp.int32, (8, 128), 1)
    sub = lax.broadcasted_iota(jnp.int32, (8, 128), 0)
    src = gram
    for p in range(panels):
        r0 = p * PANEL
        first, lane0 = r0 // 128, r0 % 128
        used = range(first, n // 128)
        tiles = []
        for t in range(PANEL // 8):
            row = src[r0 + 8 * t : r0 + 8 * t + 8, :]
            unit = jnp.where(lane == sub + 8 * t, 1.0, 0.0).astype(F32)
            tiles.append([row[:, 128 * v : 128 * v + 128] for v in used] + [unit])
        out = eliminate(tiles, lane0)
        rows = [jnp.concatenate([o[v] for o in out], axis=0) for v in range(len(used))]
        corner = jnp.concatenate([o[-1] for o in out], axis=0)[:, :PANEL]
        rows = [jnp.zeros((PANEL, 128), F32)] * first + rows
        u = jnp.concatenate(rows, axis=1)
        row_id = lax.broadcasted_iota(jnp.int32, (PANEL, n), 0) + r0
        col_id = lax.broadcasted_iota(jnp.int32, (PANEL, n), 1)
        u = jnp.where(col_id >= row_id, u, 0.0)
        work[r0 : r0 + PANEL, :] = u
        upper[r0 : r0 + PANEL, :] = u * (1.0 / scale)
        for q0 in range(r0 + PANEL, n, PANEL):
            update = exact_dot(u[:, q0 : q0 + PANEL], u, ((0,), (0,)))
            work[q0 : q0 + PANEL, :] = src[q0 : q0 + PANEL, :] - update
        src = work
        right = jnp.where(col_id == row_id, 1.0, 0.0).astype(F32)
        if p:
            right = right - exact_dot(work[0:r0, r0 : r0 + PANEL], inverse[0:r0, :], ((0,), (0,)))
        inverse[r0 : r0 + PANEL, :] = exact_dot(corner, right, ((1,), (0,)))
    turned = inverse[...].T * scale
    high[...] = turned.astype(BF16)
    low[...] = (turned - high[...].astype(F32)).astype(BF16)


def cholesky_and_inverse(gram, scale):
    n = gram.shape[0]
    full, half = (jax.ShapeDtypeStruct((n, n), t) for t in (F32, BF16))
    return pl.pallas_call(
        functools.partial(factor_kernel, scale),
        in_specs=[in_vmem()],
        out_specs=[in_vmem()] * 3,
        out_shape=(full, half, half),
        scratch_shapes=[pltpu.VMEM((n, n), F32)] * 2,
        compiler_params=params(8),
        name="cholesky_and_inverse",
    )(gram)


def basis_kernel(image, high, low, out):
    x = image[0, :, 0].reshape(out.shape)
    x_high = x.astype(BF16)
    x_low = (x - x_high.astype(F32)).astype(BF16)
    dot = functools.partial(jnp.dot, preferred_element_type=F32)
    out[...] = dot(x_high, high[...]) + (dot(x_high, low[...]) + dot(x_low, high[...]))


def make_basis(image, high, low):
    rows, width = image.shape[-2:]
    view = image.reshape(2, 4, 2, rows, width)
    return pl.pallas_call(
        basis_kernel,
        grid=(2, 2),
        in_specs=[
            pl.BlockSpec((1, 4, 1, rows, width), lambda h, o: (h, 0, o, 0, 0)),
            in_vmem(),
            in_vmem(),
        ],
        out_specs=pl.BlockSpec((4 * rows, width), lambda h, o: (2 * h + o, 0)),
        out_shape=jax.ShapeDtypeStruct((16 * rows, width), F32),
        compiler_params=params(60),
        name="make_basis",
    )(view, high, low)


def paired(value, axis, first):
    pairs = [(i, i + 1) for i in range(first, lax.axis_size(axis) - 1, 2)]
    return lax.ppermute(value, axis, pairs + [(j, i) for i, j in pairs])


def body(probes, weights, columns):
    rows, width = probes.shape
    w_local = weights[0]
    blocks, _, bs, _ = w_local.shape
    far = paired(probes, "brick", 1)
    near = paired(probes, "brick", 0)
    shape = (blocks, bs, width)
    core = jnp.full((1,), lax.axis_index("brick") % 2, jnp.int32)
    own, to_far, to_near = apply_operator(
        columns.reshape(-1), core, w_local, far.reshape(shape), probes.reshape(shape), near.reshape(shape)
    )
    from_far = paired(to_far, "brick", 1)
    from_near = paired(to_near, "brick", 0)

    zh, zp = lax.axis_index("zh"), lax.axis_index("zp")
    odd = jnp.full((1,), zp, jnp.int32)
    keep_a, send_a, keep_b, send_b = split_halves(odd, own, from_far, from_near)
    n = lax.axis_size("zh") * lax.axis_size("zp")
    got_a = lax.ppermute(send_a, DEPTH, [(i, i ^ 1) for i in range(n)])
    got_b = lax.ppermute(send_b, DEPTH, [(i, (((i + 1) ^ 1) - 1) % n) for i in range(n)])
    pieces = lax.all_to_all(add_pairs(keep_a, got_a, keep_b, got_b), "zh", 0, 0)
    block = (zh // 4) * 8 + zp * 4 + zh % 4
    image = make_image(jnp.full((1,), block, jnp.int32), pieces, probes)
    whole_image = lax.all_gather(image, DEPTH)
    gram = make_gram(image)

    bricks = lax.axis_size("brick")
    share = lax.all_to_all(gram.reshape(bricks, width // bricks, width), "brick", 0, 0)
    share = lax.all_to_all(spread_sum(share, n), DEPTH, 0, 0)
    gram = lax.all_to_all(spread_sum(share, bricks), "brick", 0, 0).reshape(width, width)

    scale = math.sqrt(rows * bricks)
    upper, high, low = cholesky_and_inverse(gram, scale)
    return make_basis(whole_image, high, low), upper


def solution(mesh):
    deep = mesh.devices.reshape(mesh.devices.shape[0] // 2, 2, mesh.devices.shape[1])
    mesh = Mesh(deep, DEPTH + ("brick",))
    in_specs = (P("brick", None), P(DEPTH, "brick", None, None, None), P(DEPTH, "brick", None))
    out_specs = (P("brick", None), P())
    return jax.shard_map(body, mesh=mesh, in_specs=in_specs, out_specs=out_specs, check_vma=False)
```

```python
import functools
import math

import jax
import jax.numpy as jnp
from jax import lax
from jax.experimental import pallas as pl
from jax.experimental.pallas import tpu as pltpu
from jax.sharding import Mesh
from jax.sharding import PartitionSpec as P

F32 = jnp.float32
BF16 = jnp.bfloat16
PANEL = 64
MIB = 1024 * 1024
DEPTH = ("zh", "zp")


def exact_dot(a, b, dims):
    return lax.dot_general(
        a, b, (dims, ((), ())), precision=lax.Precision.HIGHEST, preferred_element_type=F32
    )


def in_vmem():
    return pl.BlockSpec(memory_space=pltpu.VMEM)


def params(mib):
    return pltpu.CompilerParams(vmem_limit_bytes=mib * MIB)


def places(cols, r, blocks):
    ids = [cols[3 * r + j] for j in range(3)]
    at_low = jnp.where(ids[0] < blocks, 0, jnp.where(ids[1] < blocks, 1, 2))
    at_high = jnp.where(ids[0] >= 2 * blocks, 0, jnp.where(ids[1] >= 2 * blocks, 1, 2))
    at_own = 3 - at_low - at_high
    low, high = cols[3 * r + at_low], cols[3 * r + at_high] - 2 * blocks
    first = lax.axis_index("brick") % 2 == 0
    at = (jnp.where(first, at_low, at_high), at_own, jnp.where(first, at_high, at_low))
    return at, jnp.where(first, low, high), jnp.where(first, high, low)


def own_kernel(cols, w_ref, own_ref, w_out, data_out):
    blocks = own_ref.shape[0]

    def step(r, carry):
        at, _, _ = places(cols, r, blocks)
        for j in range(3):
            w_out[r, j] = w_ref[r, at[j]]
        data_out[r] = jnp.dot(w_ref[r, at[1]], own_ref[r], preferred_element_type=F32)
        return carry

    lax.fori_loop(0, blocks, step, 0)


def start_operator(cols, weights, own):
    blocks, slots, bs, _ = weights.shape
    width = own.shape[-1]
    return pl.pallas_call(
        own_kernel,
        in_specs=[pl.BlockSpec(memory_space=pltpu.SMEM), in_vmem(), in_vmem()],
        out_specs=[in_vmem()] * 2,
        out_shape=(
            jax.ShapeDtypeStruct(weights.shape, BF16),
            jax.ShapeDtypeStruct((blocks, bs, width), F32),
        ),
        compiler_params=params(14),
        cost_estimate=pl.CostEstimate(
            flops=2 * blocks * bs * bs * width, bytes_accessed=9 * MIB, transcendentals=0
        ),
        name="own_data",
    )(cols, weights, own)


def operator_kernel(cols, w_ref, data_ref, far_ref, near_ref, own_out, far_out, near_out, s_far, s_near, d_ref):
    blocks, _, bs, _ = w_ref.shape
    dot = functools.partial(jnp.dot, preferred_element_type=F32)
    s_far[...] = jnp.zeros_like(s_far)
    s_near[...] = jnp.zeros_like(s_near)

    def data_of(r):
        _, far, near = places(cols, r, blocks)
        w = jnp.concatenate([w_ref[r, 0], w_ref[r, 2]], axis=1)
        probes = jnp.concatenate([far_ref[far], near_ref[near]], axis=0)
        return (data_ref[r] + dot(w, probes)).astype(BF16).T

    def put(r):
        _, far, near = places(cols, r, blocks)
        w = jnp.concatenate([w_ref[r, j] for j in range(3)], axis=1)
        terms = dot(d_ref[r % 2], w)
        own_out[2 * r] = terms[:, bs : bs + 128]
        own_out[2 * r + 1] = terms[:, bs + 128 : 2 * bs]
        s_far[far] += terms[:, :bs]
        s_near[near] += terms[:, 2 * bs :]

    d_ref[0] = data_of(0)

    def step(r, carry):
        later = data_of(r + 1)
        put(r)
        d_ref[(r + 1) % 2] = later
        return carry

    lax.fori_loop(0, blocks - 1, step, 0)
    put(blocks - 1)
    for field, out in ((s_far, far_out), (s_near, near_out)):
        for q in range(blocks):
            out[2 * q] = field[q, :, :128].astype(BF16)
            out[2 * q + 1] = field[q, :, 128:].astype(BF16)


def finish_operator(cols, weights, data, far, near):
    blocks, _, bs, _ = weights.shape
    width = data.shape[-1]
    shape = (2 * blocks, width, bs // 2)
    field = pltpu.VMEM((blocks, width, bs), F32)
    return pl.pallas_call(
        operator_kernel,
        in_specs=[pl.BlockSpec(memory_space=pltpu.SMEM)] + [in_vmem()] * 4,
        out_specs=[in_vmem()] * 3,
        out_shape=(
            jax.ShapeDtypeStruct(shape, F32),
            jax.ShapeDtypeStruct(shape, BF16),
            jax.ShapeDtypeStruct(shape, BF16),
        ),
        scratch_shapes=[field, field, pltpu.VMEM((2, width, bs), BF16)],
        compiler_params=params(20),
        name="normal_operator",
    )(cols, weights, data, far, near)


def halves_kernel(own, far, near, keep, send):
    odd = lax.axis_index("zp")
    for out, parity in ((keep, odd), (send, 1 - odd)):
        for i in range(out.shape[0]):
            p = 2 * i + parity
            out[i] = (own[p] + (far[p].astype(F32) + near[p].astype(F32))).astype(out.dtype)


def split_halves(own, far, near):
    pieces, width, cells = own.shape
    kept, sent = (jax.ShapeDtypeStruct((pieces // 2, width, cells), t) for t in (F32, BF16))
    return pl.pallas_call(
        halves_kernel,
        in_specs=[in_vmem()] * 3,
        out_specs=[in_vmem()] * 2,
        out_shape=(kept, sent),
        compiler_params=params(12),
        name="split_halves",
    )(own, far, near)


def pair_kernel(keep, got, out):
    for i in range(out.shape[0]):
        out[i] = (keep[i] + got[i].astype(F32)).astype(BF16)


def add_pair(keep, got):
    return pl.pallas_call(
        pair_kernel,
        in_specs=[in_vmem()] * 2,
        out_specs=in_vmem(),
        out_shape=jax.ShapeDtypeStruct(keep.shape, BF16),
        compiler_params=params(8),
        name="add_pair",
    )(keep, got)


def image_kernel(pieces, probes, image, own, sem):
    rows = own.shape[0]
    block = 2 * lax.axis_index("zh") + lax.axis_index("zp")
    copy = pltpu.make_async_copy(probes.at[pl.ds(block * rows, rows)], own, sem)
    copy.start()
    total = pieces[0].astype(F32)
    for k in range(1, pieces.shape[0]):
        total = total + pieces[k].astype(F32)
    copy.wait()
    image[...] = own[...].astype(F32) + total.T


def make_image(pieces, probes):
    _, width, cells = pieces.shape
    return pl.pallas_call(
        image_kernel,
        in_specs=[in_vmem(), pl.BlockSpec(memory_space=pltpu.HBM)],
        out_specs=in_vmem(),
        out_shape=jax.ShapeDtypeStruct((cells, width), F32),
        scratch_shapes=[pltpu.VMEM((cells, width), BF16), pltpu.SemaphoreType.DMA],
        compiler_params=params(4),
        name="make_image",
    )(pieces, probes)


def gram_kernel(image, gram):
    gram[...] = exact_dot(image[...], image[...], ((0,), (0,)))


def make_gram(image):
    width = image.shape[1]
    return pl.pallas_call(
        gram_kernel,
        in_specs=[in_vmem()],
        out_specs=in_vmem(),
        out_shape=jax.ShapeDtypeStruct((width, width), F32),
        compiler_params=params(8),
        name="make_gram",
    )(image)


def spread_sum_kernel(pieces, out):
    total = pieces[0]
    for k in range(1, pieces.shape[0]):
        total = total + pieces[k]
    for k in range(out.shape[0]):
        out[k] = total


def spread_sum(pieces, copies):
    return pl.pallas_call(
        spread_sum_kernel,
        in_specs=[in_vmem()],
        out_specs=in_vmem(),
        out_shape=jax.ShapeDtypeStruct((copies,) + pieces.shape[1:], F32),
        compiler_params=params(4),
        name="spread_sum",
    )(pieces)


def eliminate(tiles, lane0):
    count, wide = len(tiles), len(tiles[0])
    sub = lax.broadcasted_iota(jnp.int32, (8, 128), 0)
    out = []
    for j in range(count):
        head = tiles[j]

        def columns(tile):
            first = lane0 + 8 * j
            return [
                jnp.broadcast_to(tile[0][:, first + k : first + k + 1], (8, 128)) for k in range(8)
            ]

        cols = columns(head)
        s = [[jnp.broadcast_to(cols[k][i : i + 1, :], (8, 128)) for k in range(i + 1)] for i in range(8)]
        low = [[None] * 8 for _ in range(8)]
        inv = [None] * 8
        for k in range(8):
            inv[k] = lax.rsqrt(s[k][k])
            for i in range(k + 1, 8):
                low[i][k] = s[i][k] * inv[k]
            for i in range(k + 1, 8):
                for m in range(k + 1, i + 1):
                    s[i][m] = s[i][m] - low[i][k] * low[m][k]
        u = []
        for i in range(8):
            parts = []
            for v in range(wide):
                a = jnp.broadcast_to(head[v][i : i + 1, :], (8, 128))
                for k in range(i):
                    a = a - low[i][k] * u[k][v]
                parts.append(a * inv[i])
            u.append(parts)
        rows = []
        for v in range(wide):
            t = u[0][v]
            for i in range(1, 8):
                t = jnp.where(sub == i, u[i][v], t)
            rows.append(t)
        out.append(rows)
        for r in range(j + 1, count):
            c = columns(tiles[r])
            l = []
            for i in range(8):
                a = c[i]
                for k in range(i):
                    a = a - low[i][k] * l[k]
                l.append(a * inv[i])
            new = []
            for v in range(wide):
                t = tiles[r][v]
                for i in range(8):
                    t = t - l[i] * u[i][v]
                new.append(t)
            tiles[r] = new
    return out


def factor_kernel(scale, gram, upper, high, low, work, inverse):
    n = gram.shape[0]
    panels = n // PANEL
    lane = lax.broadcasted_iota(jnp.int32, (8, 128), 1)
    sub = lax.broadcasted_iota(jnp.int32, (8, 128), 0)
    src = gram
    for p in range(panels):
        r0 = p * PANEL
        first, lane0 = r0 // 128, r0 % 128
        used = range(first, n // 128)
        tiles = []
        for t in range(PANEL // 8):
            row = src[r0 + 8 * t : r0 + 8 * t + 8, :]
            unit = jnp.where(lane == sub + 8 * t, 1.0, 0.0).astype(F32)
            tiles.append([row[:, 128 * v : 128 * v + 128] for v in used] + [unit])
        out = eliminate(tiles, lane0)
        rows = [jnp.concatenate([o[v] for o in out], axis=0) for v in range(len(used))]
        corner = jnp.concatenate([o[-1] for o in out], axis=0)[:, :PANEL]
        rows = [jnp.zeros((PANEL, 128), F32)] * first + rows
        u = jnp.concatenate(rows, axis=1)
        row_id = lax.broadcasted_iota(jnp.int32, (PANEL, n), 0) + r0
        col_id = lax.broadcasted_iota(jnp.int32, (PANEL, n), 1)
        u = jnp.where(col_id >= row_id, u, 0.0)
        work[r0 : r0 + PANEL, :] = u
        upper[r0 : r0 + PANEL, :] = u * (1.0 / scale)
        for q0 in range(r0 + PANEL, n, PANEL):
            update = exact_dot(u[:, q0 : q0 + PANEL], u, ((0,), (0,)))
            work[q0 : q0 + PANEL, :] = src[q0 : q0 + PANEL, :] - update
        src = work
        right = jnp.where(col_id == row_id, 1.0, 0.0).astype(F32)
        if p:
            right = right - exact_dot(work[0:r0, r0 : r0 + PANEL], inverse[0:r0, :], ((0,), (0,)))
        inverse[r0 : r0 + PANEL, :] = exact_dot(corner, right, ((1,), (0,)))
    turned = inverse[...].T * scale
    high[...] = turned.astype(BF16)
    low[...] = (turned - high[...].astype(F32)).astype(BF16)


def cholesky_and_inverse(gram, scale):
    n = gram.shape[0]
    full, half = (jax.ShapeDtypeStruct((n, n), t) for t in (F32, BF16))
    return pl.pallas_call(
        functools.partial(factor_kernel, scale),
        in_specs=[in_vmem()],
        out_specs=[in_vmem()] * 3,
        out_shape=(full, half, half),
        scratch_shapes=[pltpu.VMEM((n, n), F32)] * 2,
        compiler_params=params(8),
        name="cholesky_and_inverse",
    )(gram)


def basis_kernel(image, high, low, out):
    x = image[...]
    x_high = x.astype(BF16)
    x_low = (x - x_high.astype(F32)).astype(BF16)
    dot = functools.partial(jnp.dot, preferred_element_type=F32)
    out[...] = dot(x_high, high[...]) + (dot(x_high, low[...]) + dot(x_low, high[...]))


def make_basis(image, high, low):
    rows, width = image.shape
    half = pl.BlockSpec((rows // 2, width), lambda h: (h, 0))
    return pl.pallas_call(
        basis_kernel,
        grid=(2,),
        in_specs=[half, in_vmem(), in_vmem()],
        out_specs=half,
        out_shape=jax.ShapeDtypeStruct((rows, width), F32),
        compiler_params=params(60),
        name="make_basis",
    )(image, high, low)


def paired(value, axis, first):
    pairs = [(i, i + 1) for i in range(first, lax.axis_size(axis) - 1, 2)]
    return lax.ppermute(value, axis, pairs + [(j, i) for i, j in pairs])


def body(probes, weights, columns):
    rows, width = probes.shape
    w_local = weights[0]
    blocks, _, bs, _ = w_local.shape
    far = paired(probes, "brick", 1)
    near = paired(probes, "brick", 0)
    shape = (blocks, bs, width)
    cols = columns.reshape(-1)
    w_sorted, own_data = start_operator(cols, w_local, probes.reshape(shape))
    own, to_far, to_near = finish_operator(cols, w_sorted, own_data, far.reshape(shape), near.reshape(shape))
    from_far = paired(to_far, "brick", 1)
    from_near = paired(to_near, "brick", 0)

    n = lax.axis_size("zh") * lax.axis_size("zp")
    keep, send = split_halves(own, from_far, from_near)
    got = lax.ppermute(send, DEPTH, [(i, i ^ 1) for i in range(n)])
    image = make_image(lax.all_to_all(add_pair(keep, got), "zh", 0, 0), probes)
    whole_image = lax.all_gather(image, DEPTH, tiled=True)
    gram = make_gram(image)

    bricks = lax.axis_size("brick")
    share = lax.all_to_all(gram.reshape(bricks, width // bricks, width), "brick", 0, 0)
    share = lax.all_to_all(spread_sum(share, n), DEPTH, 0, 0)
    gram = lax.all_to_all(spread_sum(share, bricks), "brick", 0, 0).reshape(width, width)

    scale = math.sqrt(rows * bricks)
    upper, high, low = cholesky_and_inverse(gram, scale)
    return make_basis(whole_image, high, low), upper


def solution(mesh):
    deep = mesh.devices.reshape(mesh.devices.shape[0] // 2, 2, mesh.devices.shape[1])
    mesh = Mesh(deep, DEPTH + ("brick",))
    in_specs = (P("brick", None), P(DEPTH, "brick", None, None, None), P(DEPTH, "brick", None))
    out_specs = (P("brick", None), P())
    return jax.shard_map(body, mesh=mesh, in_specs=in_specs, out_specs=out_specs, check_vma=False)
```

```python
import functools
import math

import jax
import jax.numpy as jnp
from jax import lax
from jax.experimental import pallas as pl
from jax.experimental.pallas import tpu as pltpu
from jax.sharding import Mesh
from jax.sharding import PartitionSpec as P

F32 = jnp.float32
BF16 = jnp.bfloat16
PANEL = 64
MIB = 1024 * 1024
DEPTH = ("zh", "zp")
TAIL = 16
CODE_TOP = 32000.0


def exact_dot(a, b, dims):
    return lax.dot_general(
        a, b, (dims, ((), ())), precision=lax.Precision.HIGHEST, preferred_element_type=F32
    )


def in_vmem():
    return pl.BlockSpec(memory_space=pltpu.VMEM)


def params(mib):
    return pltpu.CompilerParams(vmem_limit_bytes=mib * MIB)


def places(cols, r, blocks):
    ids = [cols[3 * r + j] for j in range(3)]
    at_low = jnp.where(ids[0] < blocks, 0, jnp.where(ids[1] < blocks, 1, 2))
    at_high = jnp.where(ids[0] >= 2 * blocks, 0, jnp.where(ids[1] >= 2 * blocks, 1, 2))
    at_own = 3 - at_low - at_high
    low, high = cols[3 * r + at_low], cols[3 * r + at_high] - 2 * blocks
    first = lax.axis_index("brick") % 2 == 0
    at = (jnp.where(first, at_low, at_high), at_own, jnp.where(first, at_high, at_low))
    return at, jnp.where(first, low, high), jnp.where(first, high, low)


def own_kernel(cols, w_ref, own_ref, w_out, data_out):
    blocks = own_ref.shape[0]

    def step(r, carry):
        at, _, _ = places(cols, r, blocks)
        for j in range(3):
            w_out[r, j] = w_ref[r, at[j]]
        data_out[r] = jnp.dot(w_ref[r, at[1]], own_ref[r], preferred_element_type=F32)
        return carry

    lax.fori_loop(0, blocks, step, 0)


def start_operator(cols, weights, own):
    blocks, slots, bs, _ = weights.shape
    width = own.shape[-1]
    return pl.pallas_call(
        own_kernel,
        in_specs=[pl.BlockSpec(memory_space=pltpu.SMEM), in_vmem(), in_vmem()],
        out_specs=[in_vmem()] * 2,
        out_shape=(
            jax.ShapeDtypeStruct(weights.shape, BF16),
            jax.ShapeDtypeStruct((blocks, bs, width), F32),
        ),
        compiler_params=params(14),
        cost_estimate=pl.CostEstimate(
            flops=2 * blocks * bs * bs * width, bytes_accessed=9 * MIB, transcendentals=0
        ),
        name="own_data",
    )(cols, weights, own)


def operator_kernel(cols, w_ref, data_ref, far_ref, near_ref, own_out, far_out, near_out, s_far, s_near, d_ref):
    blocks, _, bs, _ = w_ref.shape
    dot = functools.partial(jnp.dot, preferred_element_type=F32)
    s_far[...] = jnp.zeros_like(s_far)
    s_near[...] = jnp.zeros_like(s_near)

    def data_of(r):
        _, far, near = places(cols, r, blocks)
        w = jnp.concatenate([w_ref[r, 0], w_ref[r, 2]], axis=1)
        probes = jnp.concatenate([far_ref[far], near_ref[near]], axis=0)
        return (data_ref[r] + dot(w, probes)).astype(BF16).T

    def put(r):
        _, far, near = places(cols, r, blocks)
        w = jnp.concatenate([w_ref[r, j] for j in range(3)], axis=1)
        terms = dot(d_ref[r % 2], w)
        own_out[2 * r] = terms[:, bs : bs + 128]
        own_out[2 * r + 1] = terms[:, bs + 128 : 2 * bs]
        s_far[far] += terms[:, :bs]
        s_near[near] += terms[:, 2 * bs :]

    d_ref[0] = data_of(0)

    def step(r, carry):
        later = data_of(r + 1)
        put(r)
        d_ref[(r + 1) % 2] = later
        return carry

    lax.fori_loop(0, blocks - 1, step, 0)
    put(blocks - 1)
    for field, out in ((s_far, far_out), (s_near, near_out)):
        for q in range(blocks):
            out[2 * q] = field[q, :, :128].astype(BF16)
            out[2 * q + 1] = field[q, :, 128:].astype(BF16)


def finish_operator(cols, weights, data, far, near):
    blocks, _, bs, _ = weights.shape
    width = data.shape[-1]
    shape = (2 * blocks, width, bs // 2)
    field = pltpu.VMEM((blocks, width, bs), F32)
    return pl.pallas_call(
        operator_kernel,
        in_specs=[pl.BlockSpec(memory_space=pltpu.SMEM)] + [in_vmem()] * 4,
        out_specs=[in_vmem()] * 3,
        out_shape=(
            jax.ShapeDtypeStruct(shape, F32),
            jax.ShapeDtypeStruct(shape, BF16),
            jax.ShapeDtypeStruct(shape, BF16),
        ),
        scratch_shapes=[field, field, pltpu.VMEM((2, width, bs), BF16)],
        compiler_params=params(20),
        name="normal_operator",
    )(cols, weights, data, far, near)


def halves_kernel(own, far, near, keep, send):
    odd = lax.axis_index("zp")
    for out, parity in ((keep, odd), (send, 1 - odd)):
        for i in range(out.shape[0]):
            p = 2 * i + parity
            out[i] = (own[p] + (far[p].astype(F32) + near[p].astype(F32))).astype(out.dtype)


def split_halves(own, far, near):
    pieces, width, cells = own.shape
    kept, sent = (jax.ShapeDtypeStruct((pieces // 2, width, cells), t) for t in (F32, BF16))
    return pl.pallas_call(
        halves_kernel,
        in_specs=[in_vmem()] * 3,
        out_specs=[in_vmem()] * 2,
        out_shape=(kept, sent),
        compiler_params=params(12),
        name="split_halves",
    )(own, far, near)


def pair_kernel(keep, got, out):
    for i in range(out.shape[0]):
        out[i] = (keep[i] + got[i].astype(F32)).astype(BF16)


def add_pair(keep, got):
    return pl.pallas_call(
        pair_kernel,
        in_specs=[in_vmem()] * 2,
        out_specs=in_vmem(),
        out_shape=jax.ShapeDtypeStruct(keep.shape, BF16),
        compiler_params=params(8),
        name="add_pair",
    )(keep, got)


def image_kernel(pieces, probes, image, coded, own, sem):
    rows = own.shape[0]
    block = 2 * lax.axis_index("zh") + lax.axis_index("zp")
    copy = pltpu.make_async_copy(probes.at[pl.ds(block * rows, rows)], own, sem)
    copy.start()
    total = pieces[0].astype(F32)
    for k in range(1, pieces.shape[0]):
        total = total + pieces[k].astype(F32)
    copy.wait()
    x = own[...].astype(F32) + total.T
    image[...] = x
    top = jnp.maximum(jnp.max(jnp.abs(x), axis=0, keepdims=True), 1e-30)
    power = jnp.ceil(jnp.log(top) * (1.0 / math.log(2.0)))
    whole = jnp.floor(x * (jnp.exp2(-power) * CODE_TOP) + 0.5)
    coded[:rows] = whole.astype(jnp.int32).astype(jnp.int16)
    tail = jnp.broadcast_to(power, (TAIL, x.shape[1]))
    coded[rows:] = tail.astype(jnp.int32).astype(jnp.int16)


def make_image(pieces, probes):
    _, width, cells = pieces.shape
    return pl.pallas_call(
        image_kernel,
        in_specs=[in_vmem(), pl.BlockSpec(memory_space=pltpu.HBM)],
        out_specs=[in_vmem()] * 2,
        out_shape=(
            jax.ShapeDtypeStruct((cells, width), F32),
            jax.ShapeDtypeStruct((cells + TAIL, width), jnp.int16),
        ),
        scratch_shapes=[pltpu.VMEM((cells, width), BF16), pltpu.SemaphoreType.DMA],
        compiler_params=params(4),
        name="make_image",
    )(pieces, probes)


def gram_kernel(image, gram):
    gram[...] = exact_dot(image[...], image[...], ((0,), (0,)))


def make_gram(image):
    width = image.shape[1]
    return pl.pallas_call(
        gram_kernel,
        in_specs=[in_vmem()],
        out_specs=in_vmem(),
        out_shape=jax.ShapeDtypeStruct((width, width), F32),
        compiler_params=params(8),
        name="make_gram",
    )(image)


def spread_sum_kernel(pieces, held, got, out, joined):
    total = pieces[0]
    for k in range(1, pieces.shape[0]):
        total = total + pieces[k]
    for k in range(out.shape[0]):
        out[k] = total
    copy_both(held, got, joined)


def spread_sum(pieces, copies, held, got):
    count = held.shape[0]
    return pl.pallas_call(
        spread_sum_kernel,
        in_specs=[in_vmem()] * 3,
        out_specs=[in_vmem()] * 2,
        out_shape=(
            jax.ShapeDtypeStruct((copies,) + pieces.shape[1:], F32),
            jax.ShapeDtypeStruct((2 * count,) + held.shape[1:], held.dtype),
        ),
        compiler_params=params(6),
        name="spread_sum",
    )(pieces, held, got)


def copy_both(held, got, joined):
    count = held.shape[0]
    joined[:count] = held[...]
    joined[count:] = got[...]


def join_kernel(held, got, gram, joined):
    copy_both(held, got, joined)


def join(held, got, gram):
    return pl.pallas_call(
        join_kernel,
        in_specs=[in_vmem()] * 2 + [pl.BlockSpec(memory_space=pl.ANY)],
        out_specs=in_vmem(),
        out_shape=jax.ShapeDtypeStruct((2 * held.shape[0],) + held.shape[1:], held.dtype),
        compiler_params=params(6),
        name="join",
    )(held, got, gram)


def eliminate(tiles, lane0):
    count, wide = len(tiles), len(tiles[0])
    sub = lax.broadcasted_iota(jnp.int32, (8, 128), 0)
    out = []
    for j in range(count):
        head = tiles[j]

        def columns(tile):
            first = lane0 + 8 * j
            return [
                jnp.broadcast_to(tile[0][:, first + k : first + k + 1], (8, 128)) for k in range(8)
            ]

        cols = columns(head)
        s = [[jnp.broadcast_to(cols[k][i : i + 1, :], (8, 128)) for k in range(i + 1)] for i in range(8)]
        low = [[None] * 8 for _ in range(8)]
        inv = [None] * 8
        for k in range(8):
            inv[k] = lax.rsqrt(s[k][k])
            for i in range(k + 1, 8):
                low[i][k] = s[i][k] * inv[k]
            for i in range(k + 1, 8):
                for m in range(k + 1, i + 1):
                    s[i][m] = s[i][m] - low[i][k] * low[m][k]
        u = []
        for i in range(8):
            parts = []
            for v in range(wide):
                a = jnp.broadcast_to(head[v][i : i + 1, :], (8, 128))
                for k in range(i):
                    a = a - low[i][k] * u[k][v]
                parts.append(a * inv[i])
            u.append(parts)
        rows = []
        for v in range(wide):
            t = u[0][v]
            for i in range(1, 8):
                t = jnp.where(sub == i, u[i][v], t)
            rows.append(t)
        out.append(rows)
        for r in range(j + 1, count):
            c = columns(tiles[r])
            l = []
            for i in range(8):
                a = c[i]
                for k in range(i):
                    a = a - low[i][k] * l[k]
                l.append(a * inv[i])
            new = []
            for v in range(wide):
                t = tiles[r][v]
                for i in range(8):
                    t = t - l[i] * u[i][v]
                new.append(t)
            tiles[r] = new
    return out


def factor_kernel(scale, gram, upper, high, low, work, inverse):
    n = gram.shape[0]
    panels = n // PANEL
    lane = lax.broadcasted_iota(jnp.int32, (8, 128), 1)
    sub = lax.broadcasted_iota(jnp.int32, (8, 128), 0)
    src = gram
    for p in range(panels):
        r0 = p * PANEL
        first, lane0 = r0 // 128, r0 % 128
        used = range(first, n // 128)
        tiles = []
        for t in range(PANEL // 8):
            row = src[r0 + 8 * t : r0 + 8 * t + 8, :]
            unit = jnp.where(lane == sub + 8 * t, 1.0, 0.0).astype(F32)
            tiles.append([row[:, 128 * v : 128 * v + 128] for v in used] + [unit])
        out = eliminate(tiles, lane0)
        rows = [jnp.concatenate([o[v] for o in out], axis=0) for v in range(len(used))]
        corner = jnp.concatenate([o[-1] for o in out], axis=0)[:, :PANEL]
        rows = [jnp.zeros((PANEL, 128), F32)] * first + rows
        u = jnp.concatenate(rows, axis=1)
        row_id = lax.broadcasted_iota(jnp.int32, (PANEL, n), 0) + r0
        col_id = lax.broadcasted_iota(jnp.int32, (PANEL, n), 1)
        u = jnp.where(col_id >= row_id, u, 0.0)
        work[r0 : r0 + PANEL, :] = u
        upper[r0 : r0 + PANEL, :] = u * (1.0 / scale)
        for q0 in range(r0 + PANEL, n, PANEL):
            update = exact_dot(u[:, q0 : q0 + PANEL], u, ((0,), (0,)))
            work[q0 : q0 + PANEL, :] = src[q0 : q0 + PANEL, :] - update
        src = work
        right = jnp.where(col_id == row_id, 1.0, 0.0).astype(F32)
        if p:
            right = right - exact_dot(work[0:r0, r0 : r0 + PANEL], inverse[0:r0, :], ((0,), (0,)))
        inverse[r0 : r0 + PANEL, :] = exact_dot(corner, right, ((1,), (0,)))
    turned = inverse[...].T * scale
    high[...] = turned.astype(BF16)
    low[...] = (turned - high[...].astype(F32)).astype(BF16)


def cholesky_and_inverse(gram, scale):
    n = gram.shape[0]
    full, half = (jax.ShapeDtypeStruct((n, n), t) for t in (F32, BF16))
    return pl.pallas_call(
        functools.partial(factor_kernel, scale),
        in_specs=[in_vmem()],
        out_specs=[in_vmem()] * 3,
        out_shape=(full, half, half),
        scratch_shapes=[pltpu.VMEM((n, n), F32)] * 2,
        compiler_params=params(8),
        name="cholesky_and_inverse",
    )(gram)


def basis_kernel(held, got, high, low, out, staged, sems):
    count = held.shape[0]
    rows, width = staged.shape[2:]
    group = staged.shape[1]
    here = 2 * lax.axis_index("zh") + lax.axis_index("zp")
    dot = functools.partial(jnp.dot, preferred_element_type=F32)
    copies = []
    for g in range(staged.shape[0]):
        parts = []
        for i in range(group):
            k = g * group + i
            piece = (held if k < count else got).at[k % count]
            power = piece[rows:].astype(jnp.int32).astype(F32)[:1]
            parts.append(piece[:rows].astype(jnp.int32).astype(F32) * (jnp.exp2(power) * (1.0 / CODE_TOP)))
        x = jnp.concatenate(parts, axis=0)
        x_high = x.astype(BF16)
        x_low = (x - x_high.astype(F32)).astype(BF16)
        y = dot(x_high, high[...]) + (dot(x_high, low[...]) + dot(x_low, high[...]))
        staged[g] = y.reshape(group, rows, width)
        for i in range(group):
            k = g * group + i
            flip = 8 * (k & 1) + 4 * (k >> 1 & 1) + 2 * (k >> 2 & 1) + (k >> 3)
            to = pl.ds(pl.multiple_of((here ^ flip) * rows, rows), rows)
            copy = pltpu.make_async_copy(staged.at[g, i], out.at[to], sems.at[k])
            copy.start()
            copies.append(copy)
    for copy in copies:
        copy.wait()


def make_basis(held, got, high, low):
    count, rows, width = held.shape
    rows -= TAIL
    return pl.pallas_call(
        basis_kernel,
        in_specs=[in_vmem()] * 4,
        out_specs=pl.BlockSpec(memory_space=pltpu.HBM),
        out_shape=jax.ShapeDtypeStruct((2 * count * rows, width), F32),
        scratch_shapes=[
            pltpu.VMEM((4, count // 2, rows, width), F32),
            pltpu.SemaphoreType.DMA((2 * count,)),
        ],
        compiler_params=params(16),
        name="make_basis",
    )(held, got, high, low)


def paired(value, axis, first):
    pairs = [(i, i + 1) for i in range(first, lax.axis_size(axis) - 1, 2)]
    return lax.ppermute(value, axis, pairs + [(j, i) for i, j in pairs])


def body(probes, weights, columns):
    rows, width = probes.shape
    w_local = weights[0]
    blocks, _, bs, _ = w_local.shape
    far = paired(probes, "brick", 1)
    near = paired(probes, "brick", 0)
    shape = (blocks, bs, width)
    cols = columns.reshape(-1)
    w_sorted, own_data = start_operator(cols, w_local, probes.reshape(shape))
    own, to_far, to_near = finish_operator(cols, w_sorted, own_data, far.reshape(shape), near.reshape(shape))
    from_far = paired(to_far, "brick", 1)
    from_near = paired(to_near, "brick", 0)

    n = lax.axis_size("zh") * lax.axis_size("zp")
    keep, send = split_halves(own, from_far, from_near)
    got = lax.ppermute(send, DEPTH, [(i, i ^ 1) for i in range(n)])
    image, coded = make_image(lax.all_to_all(add_pair(keep, got), "zh", 0, 0), probes)

    def swap(held, distance):
        return lax.ppermute(held, DEPTH, [(i, i ^ distance) for i in range(n)])

    held = coded[None]
    got = swap(held, 8)
    gram = make_gram(image)
    bricks = lax.axis_size("brick")
    share = lax.all_to_all(gram.reshape(bricks, width // bricks, width), "brick", 0, 0)
    share, held = spread_sum(share, n, held, got)
    got = swap(held, 4)
    share = lax.all_to_all(share, DEPTH, 0, 0)
    share, held = spread_sum(share, bricks, held, got)
    got = swap(held, 2)
    gram = lax.all_to_all(share, "brick", 0, 0).reshape(width, width)
    held = join(held, got, gram)
    got = swap(held, 1)

    scale = math.sqrt(rows * bricks)
    upper, high, low = cholesky_and_inverse(gram, scale)
    return make_basis(held, got, high, low), upper


def solution(mesh):
    deep = mesh.devices.reshape(mesh.devices.shape[0] // 2, 2, mesh.devices.shape[1])
    mesh = Mesh(deep, DEPTH + ("brick",))
    in_specs = (P("brick", None), P(DEPTH, "brick", None, None, None), P(DEPTH, "brick", None))
    out_specs = (P("brick", None), P())
    return jax.shard_map(body, mesh=mesh, in_specs=in_specs, out_specs=out_specs, check_vma=False)
```

```python
import functools
import math

import jax
import jax.numpy as jnp
from jax import lax
from jax.experimental import pallas as pl
from jax.experimental.pallas import tpu as pltpu
from jax.sharding import Mesh
from jax.sharding import PartitionSpec as P

F32 = jnp.float32
BF16 = jnp.bfloat16
PANEL = 64
MIB = 1024 * 1024
DEPTH = ("za", "zb", "zc")
TAIL = 16
CODE_TOP = 32000.0


def position():
    return 4 * lax.axis_index("za") + 2 * lax.axis_index("zb") + lax.axis_index("zc")


def exact_dot(a, b, dims):
    return lax.dot_general(
        a, b, (dims, ((), ())), precision=lax.Precision.HIGHEST, preferred_element_type=F32
    )


def in_vmem():
    return pl.BlockSpec(memory_space=pltpu.VMEM)


def params(mib):
    return pltpu.CompilerParams(vmem_limit_bytes=mib * MIB)


def places(cols, r, blocks):
    ids = [cols[3 * r + j] for j in range(3)]
    at_low = jnp.where(ids[0] < blocks, 0, jnp.where(ids[1] < blocks, 1, 2))
    at_high = jnp.where(ids[0] >= 2 * blocks, 0, jnp.where(ids[1] >= 2 * blocks, 1, 2))
    at_own = 3 - at_low - at_high
    low, high = cols[3 * r + at_low], cols[3 * r + at_high] - 2 * blocks
    first = lax.axis_index("brick") % 2 == 0
    at = (jnp.where(first, at_low, at_high), at_own, jnp.where(first, at_high, at_low))
    return at, jnp.where(first, low, high), jnp.where(first, high, low)


def own_kernel(cols, w_ref, own_ref, w_out, data_out):
    blocks = own_ref.shape[0]

    def step(r, carry):
        at, _, _ = places(cols, r, blocks)
        for j in range(3):
            w_out[r, j] = w_ref[r, at[j]]
        data_out[r] = jnp.dot(w_ref[r, at[1]], own_ref[r], preferred_element_type=F32)
        return carry

    lax.fori_loop(0, blocks, step, 0)


def start_operator(cols, weights, own):
    blocks, slots, bs, _ = weights.shape
    width = own.shape[-1]
    return pl.pallas_call(
        own_kernel,
        in_specs=[pl.BlockSpec(memory_space=pltpu.SMEM), in_vmem(), in_vmem()],
        out_specs=[in_vmem()] * 2,
        out_shape=(
            jax.ShapeDtypeStruct(weights.shape, BF16),
            jax.ShapeDtypeStruct((blocks, bs, width), F32),
        ),
        compiler_params=params(14),
        cost_estimate=pl.CostEstimate(
            flops=2 * blocks * bs * bs * width, bytes_accessed=9 * MIB, transcendentals=0
        ),
        name="own_data",
    )(cols, weights, own)


def operator_kernel(cols, w_ref, data_ref, far_ref, near_ref, own_out, far_out, near_out, s_far, s_near, d_ref):
    blocks, _, bs, _ = w_ref.shape
    dot = functools.partial(jnp.dot, preferred_element_type=F32)
    s_far[...] = jnp.zeros_like(s_far)
    s_near[...] = jnp.zeros_like(s_near)

    def data_of(r):
        _, far, near = places(cols, r, blocks)
        w = jnp.concatenate([w_ref[r, 0], w_ref[r, 2]], axis=1)
        probes = jnp.concatenate([far_ref[far], near_ref[near]], axis=0)
        return (data_ref[r] + dot(w, probes)).astype(BF16).T

    def put(r):
        _, far, near = places(cols, r, blocks)
        w = jnp.concatenate([w_ref[r, j] for j in range(3)], axis=1)
        terms = dot(d_ref[r % 2], w)
        own_out[2 * r] = terms[:, bs : bs + 128]
        own_out[2 * r + 1] = terms[:, bs + 128 : 2 * bs]
        s_far[far] += terms[:, :bs]
        s_near[near] += terms[:, 2 * bs :]

    d_ref[0] = data_of(0)

    def step(r, carry):
        later = data_of(r + 1)
        put(r)
        d_ref[(r + 1) % 2] = later
        return carry

    lax.fori_loop(0, blocks - 1, step, 0)
    put(blocks - 1)
    for field, out in ((s_far, far_out), (s_near, near_out)):
        for q in range(blocks):
            out[2 * q] = field[q, :, :128].astype(BF16)
            out[2 * q + 1] = field[q, :, 128:].astype(BF16)


def finish_operator(cols, weights, data, far, near):
    blocks, _, bs, _ = weights.shape
    width = data.shape[-1]
    shape = (2 * blocks, width, bs // 2)
    field = pltpu.VMEM((blocks, width, bs), F32)
    return pl.pallas_call(
        operator_kernel,
        in_specs=[pl.BlockSpec(memory_space=pltpu.SMEM)] + [in_vmem()] * 4,
        out_specs=[in_vmem()] * 3,
        out_shape=(
            jax.ShapeDtypeStruct(shape, F32),
            jax.ShapeDtypeStruct(shape, BF16),
            jax.ShapeDtypeStruct(shape, BF16),
        ),
        scratch_shapes=[field, field, pltpu.VMEM((2, width, bs), BF16)],
        compiler_params=params(20),
        name="normal_operator",
    )(cols, weights, data, far, near)


def halves_kernel(own, far, near, keep, send):
    odd = lax.axis_index("zc")
    for out, parity in ((keep, odd), (send, 1 - odd)):
        for i in range(out.shape[0]):
            p = 2 * i + parity
            out[i] = (own[p] + (far[p].astype(F32) + near[p].astype(F32))).astype(out.dtype)


def split_halves(own, far, near):
    pieces, width, cells = own.shape
    kept, sent = (jax.ShapeDtypeStruct((pieces // 2, width, cells), t) for t in (F32, BF16))
    return pl.pallas_call(
        halves_kernel,
        in_specs=[in_vmem()] * 3,
        out_specs=[in_vmem()] * 2,
        out_shape=(kept, sent),
        compiler_params=params(12),
        name="split_halves",
    )(own, far, near)


def pair_kernel(keep, got, out):
    for i in range(out.shape[0]):
        out[i] = (keep[i] + got[i].astype(F32)).astype(BF16)


def add_pair(keep, got):
    return pl.pallas_call(
        pair_kernel,
        in_specs=[in_vmem()] * 2,
        out_specs=in_vmem(),
        out_shape=jax.ShapeDtypeStruct(keep.shape, BF16),
        compiler_params=params(8),
        name="add_pair",
    )(keep, got)


def image_kernel(pieces, probes, image, coded, own, sem):
    rows = own.shape[0]
    block = position()
    copy = pltpu.make_async_copy(probes.at[pl.ds(block * rows, rows)], own, sem)
    copy.start()
    total = pieces[0].astype(F32)
    for k in range(1, pieces.shape[0]):
        total = total + pieces[k].astype(F32)
    copy.wait()
    x = own[...].astype(F32) + total.T
    image[...] = x
    top = jnp.maximum(jnp.max(jnp.abs(x), axis=0, keepdims=True), 1e-30)
    power = jnp.ceil(jnp.log(top) * (1.0 / math.log(2.0)))
    whole = jnp.floor(x * (jnp.exp2(-power) * CODE_TOP) + 0.5)
    coded[:rows] = whole.astype(jnp.int32).astype(jnp.int16)
    tail = jnp.broadcast_to(power, (TAIL, x.shape[1]))
    coded[rows:] = tail.astype(jnp.int32).astype(jnp.int16)


def make_image(pieces, probes):
    _, width, cells = pieces.shape
    return pl.pallas_call(
        image_kernel,
        in_specs=[in_vmem(), pl.BlockSpec(memory_space=pltpu.HBM)],
        out_specs=[in_vmem()] * 2,
        out_shape=(
            jax.ShapeDtypeStruct((cells, width), F32),
            jax.ShapeDtypeStruct((cells + TAIL, width), jnp.int16),
        ),
        scratch_shapes=[pltpu.VMEM((cells, width), BF16), pltpu.SemaphoreType.DMA],
        compiler_params=params(4),
        name="make_image",
    )(pieces, probes)


def gram_kernel(image, gram):
    gram[...] = exact_dot(image[...], image[...], ((0,), (0,)))


def make_gram(image):
    width = image.shape[1]
    return pl.pallas_call(
        gram_kernel,
        in_specs=[in_vmem()],
        out_specs=in_vmem(),
        out_shape=jax.ShapeDtypeStruct((width, width), F32),
        compiler_params=params(8),
        name="make_gram",
    )(image)


def spread(pieces, out):
    total = pieces[0]
    for k in range(1, pieces.shape[0]):
        total = total + pieces[k]
    for k in range(out.shape[0]):
        out[k] = total


def spread_sum_kernel(pieces, out):
    spread(pieces, out)


def spread_sum(pieces, copies):
    return pl.pallas_call(
        spread_sum_kernel,
        in_specs=[in_vmem()],
        out_specs=in_vmem(),
        out_shape=jax.ShapeDtypeStruct((copies,) + pieces.shape[1:], F32),
        compiler_params=params(4),
        name="spread_sum",
    )(pieces)


def eliminate(tiles, lane0):
    count, wide = len(tiles), len(tiles[0])
    sub = lax.broadcasted_iota(jnp.int32, (8, 128), 0)
    out = []
    for j in range(count):
        head = tiles[j]

        def columns(tile):
            first = lane0 + 8 * j
            return [
                jnp.broadcast_to(tile[0][:, first + k : first + k + 1], (8, 128)) for k in range(8)
            ]

        cols = columns(head)
        s = [[jnp.broadcast_to(cols[k][i : i + 1, :], (8, 128)) for k in range(i + 1)] for i in range(8)]
        low = [[None] * 8 for _ in range(8)]
        inv = [None] * 8
        for k in range(8):
            inv[k] = lax.rsqrt(s[k][k])
            for i in range(k + 1, 8):
                low[i][k] = s[i][k] * inv[k]
            for i in range(k + 1, 8):
                for m in range(k + 1, i + 1):
                    s[i][m] = s[i][m] - low[i][k] * low[m][k]
        u = []
        for i in range(8):
            parts = []
            for v in range(wide):
                a = jnp.broadcast_to(head[v][i : i + 1, :], (8, 128))
                for k in range(i):
                    a = a - low[i][k] * u[k][v]
                parts.append(a * inv[i])
            u.append(parts)
        rows = []
        for v in range(wide):
            t = u[0][v]
            for i in range(1, 8):
                t = jnp.where(sub == i, u[i][v], t)
            rows.append(t)
        out.append(rows)
        for r in range(j + 1, count):
            c = columns(tiles[r])
            l = []
            for i in range(8):
                a = c[i]
                for k in range(i):
                    a = a - low[i][k] * l[k]
                l.append(a * inv[i])
            new = []
            for v in range(wide):
                t = tiles[r][v]
                for i in range(8):
                    t = t - l[i] * u[i][v]
                new.append(t)
            tiles[r] = new
    return out


def factor_kernel(scale, gram, upper, high, low, work, inverse):
    n = gram.shape[0]
    panels = n // PANEL
    lane = lax.broadcasted_iota(jnp.int32, (8, 128), 1)
    sub = lax.broadcasted_iota(jnp.int32, (8, 128), 0)
    src = gram
    for p in range(panels):
        r0 = p * PANEL
        first, lane0 = r0 // 128, r0 % 128
        used = range(first, n // 128)
        tiles = []
        for t in range(PANEL // 8):
            row = src[r0 + 8 * t : r0 + 8 * t + 8, :]
            unit = jnp.where(lane == sub + 8 * t, 1.0, 0.0).astype(F32)
            tiles.append([row[:, 128 * v : 128 * v + 128] for v in used] + [unit])
        out = eliminate(tiles, lane0)
        rows = [jnp.concatenate([o[v] for o in out], axis=0) for v in range(len(used))]
        corner = jnp.concatenate([o[-1] for o in out], axis=0)[:, :PANEL]
        rows = [jnp.zeros((PANEL, 128), F32)] * first + rows
        u = jnp.concatenate(rows, axis=1)
        row_id = lax.broadcasted_iota(jnp.int32, (PANEL, n), 0) + r0
        col_id = lax.broadcasted_iota(jnp.int32, (PANEL, n), 1)
        u = jnp.where(col_id >= row_id, u, 0.0)
        work[r0 : r0 + PANEL, :] = u
        upper[r0 : r0 + PANEL, :] = u * (1.0 / scale)
        for q0 in range(r0 + PANEL, n, PANEL):
            update = exact_dot(u[:, q0 : q0 + PANEL], u, ((0,), (0,)))
            work[q0 : q0 + PANEL, :] = src[q0 : q0 + PANEL, :] - update
        src = work
        right = jnp.where(col_id == row_id, 1.0, 0.0).astype(F32)
        if p:
            right = right - exact_dot(work[0:r0, r0 : r0 + PANEL], inverse[0:r0, :], ((0,), (0,)))
        inverse[r0 : r0 + PANEL, :] = exact_dot(corner, right, ((1,), (0,)))
    turned = inverse[...].T * scale
    high[...] = turned.astype(BF16)
    low[...] = (turned - high[...].astype(F32)).astype(BF16)


def cholesky_and_inverse(gram, scale):
    n = gram.shape[0]
    full, half = (jax.ShapeDtypeStruct((n, n), t) for t in (F32, BF16))
    return pl.pallas_call(
        functools.partial(factor_kernel, scale),
        in_specs=[in_vmem()],
        out_specs=[in_vmem()] * 3,
        out_shape=(full, half, half),
        scratch_shapes=[pltpu.VMEM((n, n), F32)] * 2,
        compiler_params=params(8),
        name="cholesky_and_inverse",
    )(gram)


def basis_kernel(*refs):
    parts, (high, low, out, staged, sems) = refs[:4], refs[4:]
    rows, width = staged.shape[2:]
    here = position()
    dot = functools.partial(jnp.dot, preferred_element_type=F32)
    copies = []
    for g, part in enumerate(parts):
        pieces = []
        for i in range(4):
            power = part[i, rows:].astype(jnp.int32).astype(F32)[:1]
            piece = part[i, :rows].astype(jnp.int32).astype(F32)
            pieces.append(piece * (jnp.exp2(power) * (1.0 / CODE_TOP)))
        x = jnp.concatenate(pieces, axis=0)
        x_high = x.astype(BF16)
        x_low = (x - x_high.astype(F32)).astype(BF16)
        y = dot(x_high, high[...]) + (dot(x_high, low[...]) + dot(x_low, high[...]))
        staged[g] = y.reshape(4, rows, width)
        for i in range(4):
            source = 4 * i + ((here % 4) ^ g)
            to = pl.ds(pl.multiple_of(source * rows, rows), rows)
            copy = pltpu.make_async_copy(staged.at[g, i], out.at[to], sems.at[4 * g + i])
            copy.start()
            copies.append(copy)
    for copy in copies:
        copy.wait()


def make_basis(parts, high, low):
    count, rows, width = parts[0].shape
    rows -= TAIL
    return pl.pallas_call(
        basis_kernel,
        in_specs=[in_vmem()] * 6,
        out_specs=pl.BlockSpec(memory_space=pltpu.HBM),
        out_shape=jax.ShapeDtypeStruct((4 * count * rows, width), F32),
        scratch_shapes=[
            pltpu.VMEM((4, count, rows, width), F32),
            pltpu.SemaphoreType.DMA((4 * count,)),
        ],
        compiler_params=params(16),
        name="make_basis",
    )(*parts, high, low)


def paired(value, axis, first):
    pairs = [(i, i + 1) for i in range(first, lax.axis_size(axis) - 1, 2)]
    return lax.ppermute(value, axis, pairs + [(j, i) for i, j in pairs])


def body(probes, weights, columns):
    rows, width = probes.shape
    w_local = weights[0]
    blocks, _, bs, _ = w_local.shape
    far = paired(probes, "brick", 1)
    near = paired(probes, "brick", 0)
    shape = (blocks, bs, width)
    cols = columns.reshape(-1)
    w_sorted, own_data = start_operator(cols, w_local, probes.reshape(shape))
    own, to_far, to_near = finish_operator(cols, w_sorted, own_data, far.reshape(shape), near.reshape(shape))
    from_far = paired(to_far, "brick", 1)
    from_near = paired(to_near, "brick", 0)

    n = lax.axis_size(DEPTH)
    keep, send = split_halves(own, from_far, from_near)

    def swap(held, distance):
        return lax.ppermute(held, DEPTH, [(i, i ^ distance) for i in range(n)])

    held = add_pair(keep, swap(send, 1))
    image, coded = make_image(lax.all_to_all(held, ("za", "zb"), 0, 0), probes)

    held = lax.all_gather(coded, "za")
    gram = make_gram(image)
    bricks = lax.axis_size("brick")
    share = lax.all_to_all(gram.reshape(bricks, width // bricks, width), "brick", 0, 0)
    share = lax.all_to_all(spread_sum(share, n), DEPTH, 0, 0)
    parts = [held] + [swap(held, k) for k in (1, 2, 3)]
    gram = lax.all_to_all(spread_sum(share, bricks), "brick", 0, 0).reshape(width, width)

    scale = math.sqrt(rows * bricks)
    upper, high, low = cholesky_and_inverse(gram, scale)
    return make_basis(parts, high, low), upper


def solution(mesh):
    deep = mesh.devices.reshape(mesh.devices.shape[0] // 4, 2, 2, mesh.devices.shape[1])
    mesh = Mesh(deep, DEPTH + ("brick",))
    in_specs = (P("brick", None), P(DEPTH, "brick", None, None, None), P(DEPTH, "brick", None))
    out_specs = (P("brick", None), P())
    return jax.shard_map(body, mesh=mesh, in_specs=in_specs, out_specs=out_specs, check_vma=False)
```

```python
import functools
import math

import jax
import jax.numpy as jnp
from jax import lax
from jax.experimental import pallas as pl
from jax.experimental.pallas import tpu as pltpu
from jax.sharding import Mesh
from jax.sharding import PartitionSpec as P

F32 = jnp.float32
BF16 = jnp.bfloat16
PANEL = 64
MIB = 1024 * 1024
DEPTH = ("za", "zb", "zc")
TAIL = 16
CODE_TOP = 32000.0


def position():
    return 4 * lax.axis_index("za") + 2 * lax.axis_index("zb") + lax.axis_index("zc")


def exact_dot(a, b, dims):
    return lax.dot_general(
        a, b, (dims, ((), ())), precision=lax.Precision.HIGHEST, preferred_element_type=F32
    )


def in_vmem():
    return pl.BlockSpec(memory_space=pltpu.VMEM)


def params(mib):
    return pltpu.CompilerParams(vmem_limit_bytes=mib * MIB)


def places(cols, r, blocks):
    ids = [cols[3 * r + j] for j in range(3)]
    at_low = jnp.where(ids[0] < blocks, 0, jnp.where(ids[1] < blocks, 1, 2))
    at_high = jnp.where(ids[0] >= 2 * blocks, 0, jnp.where(ids[1] >= 2 * blocks, 1, 2))
    at_own = 3 - at_low - at_high
    low, high = cols[3 * r + at_low], cols[3 * r + at_high] - 2 * blocks
    first = lax.axis_index("brick") % 2 == 0
    at = (jnp.where(first, at_low, at_high), at_own, jnp.where(first, at_high, at_low))
    return at, jnp.where(first, low, high), jnp.where(first, high, low)


def own_kernel(cols, w_ref, own_ref, w_out, data_out):
    blocks = own_ref.shape[0]

    def step(r, carry):
        at, _, _ = places(cols, r, blocks)
        for j in range(3):
            w_out[r, j] = w_ref[r, at[j]]
        data_out[r] = jnp.dot(w_ref[r, at[1]], own_ref[r], preferred_element_type=F32)
        return carry

    lax.fori_loop(0, blocks, step, 0)


def start_operator(cols, weights, own):
    blocks, slots, bs, _ = weights.shape
    width = own.shape[-1]
    return pl.pallas_call(
        own_kernel,
        in_specs=[pl.BlockSpec(memory_space=pltpu.SMEM), in_vmem(), in_vmem()],
        out_specs=[in_vmem()] * 2,
        out_shape=(
            jax.ShapeDtypeStruct(weights.shape, BF16),
            jax.ShapeDtypeStruct((blocks, bs, width), F32),
        ),
        compiler_params=params(14),
        cost_estimate=pl.CostEstimate(
            flops=2 * blocks * bs * bs * width, bytes_accessed=9 * MIB, transcendentals=0
        ),
        name="own_data",
    )(cols, weights, own)


def operator_kernel(
    cols, w_ref, data_ref, far_ref, near_ref, own_out, far_first, far_last, near_out, s_far, s_near, d_ref
):
    blocks, _, bs, _ = w_ref.shape
    dot = functools.partial(jnp.dot, preferred_element_type=F32)
    s_far[...] = jnp.zeros_like(s_far)
    s_near[...] = jnp.zeros_like(s_near)

    def data_of(r):
        _, far, near = places(cols, r, blocks)
        w = jnp.concatenate([w_ref[r, 0], w_ref[r, 2]], axis=1)
        probes = jnp.concatenate([far_ref[far], near_ref[near]], axis=0)
        return (data_ref[r] + dot(w, probes)).astype(BF16).T

    def put(r):
        _, far, near = places(cols, r, blocks)
        w = jnp.concatenate([w_ref[r, j] for j in range(3)], axis=1)
        terms = dot(d_ref[r % 2], w)
        own_out[2 * r] = terms[:, bs : bs + 128]
        own_out[2 * r + 1] = terms[:, bs + 128 : 2 * bs]
        s_far[far] += terms[:, :bs]
        s_near[near] += terms[:, 2 * bs :]

    d_ref[0] = data_of(0)

    def step(r, carry):
        later = data_of(r + 1)
        put(r)
        d_ref[(r + 1) % 2] = later
        return carry

    lax.fori_loop(0, blocks - 1, step, 0)
    put(blocks - 1)
    half = blocks // 2
    for q in range(blocks):
        far_out = far_first if q < half else far_last
        for out, k, field in ((far_out, q % half, s_far), (near_out, q, s_near)):
            out[2 * k] = field[q, :, :128].astype(BF16)
            out[2 * k + 1] = field[q, :, 128:].astype(BF16)


def finish_operator(cols, weights, data, far, near):
    blocks, _, bs, _ = weights.shape
    width = data.shape[-1]
    shape = (2 * blocks, width, bs // 2)
    half = jax.ShapeDtypeStruct((blocks, width, bs // 2), BF16)
    field = pltpu.VMEM((blocks, width, bs), F32)
    return pl.pallas_call(
        operator_kernel,
        in_specs=[pl.BlockSpec(memory_space=pltpu.SMEM)] + [in_vmem()] * 4,
        out_specs=[in_vmem()] * 4,
        out_shape=(
            jax.ShapeDtypeStruct(shape, F32),
            half,
            half,
            jax.ShapeDtypeStruct(shape, BF16),
        ),
        scratch_shapes=[field, field, pltpu.VMEM((2, width, bs), BF16)],
        compiler_params=params(20),
        name="normal_operator",
    )(cols, weights, data, far, near)


def parity_kernel(first, own, far, near, keep, send):
    odd = lax.axis_index("zc")
    for out, parity in ((keep, odd), (send, 1 - odd)):
        for i in range(out.shape[0]):
            p = 2 * i + parity
            total = far[p].astype(F32) + near[first + p].astype(F32)
            out[i] = (own[first + p] + total).astype(out.dtype)


def split_parity(first, own, far, near):
    pieces, width, cells = far.shape
    kept, sent = (jax.ShapeDtypeStruct((pieces // 2, width, cells), t) for t in (F32, BF16))
    return pl.pallas_call(
        functools.partial(parity_kernel, first),
        in_specs=[in_vmem()] * 3,
        out_specs=[in_vmem()] * 2,
        out_shape=(kept, sent),
        compiler_params=params(12),
        name="split_parity",
    )(own, far, near)


def pair_kernel(keep, got, keep_last, got_last, out):
    n = keep.shape[0]
    for i in range(n):
        out[i] = (keep[i] + got[i].astype(F32)).astype(BF16)
        out[n + i] = (keep_last[i] + got_last[i].astype(F32)).astype(BF16)


def add_pair(*halves):
    n, width, cells = halves[0].shape
    return pl.pallas_call(
        pair_kernel,
        in_specs=[in_vmem()] * 4,
        out_specs=in_vmem(),
        out_shape=jax.ShapeDtypeStruct((2 * n, width, cells), BF16),
        compiler_params=params(8),
        name="add_pair",
    )(*halves)


def image_kernel(pieces, probes, image, coded, own, sem):
    rows = own.shape[0]
    block = position()
    copy = pltpu.make_async_copy(probes.at[pl.ds(block * rows, rows)], own, sem)
    copy.start()
    total = pieces[0].astype(F32)
    for k in range(1, pieces.shape[0]):
        total = total + pieces[k].astype(F32)
    copy.wait()
    x = own[...].astype(F32) + total.T
    image[...] = x
    top = jnp.maximum(jnp.max(jnp.abs(x), axis=0, keepdims=True), 1e-30)
    power = jnp.ceil(jnp.log(top) * (1.0 / math.log(2.0)))
    whole = jnp.floor(x * (jnp.exp2(-power) * CODE_TOP) + 0.5)
    coded[:rows] = whole.astype(jnp.int32).astype(jnp.int16)
    tail = jnp.broadcast_to(power, (TAIL, x.shape[1]))
    coded[rows:] = tail.astype(jnp.int32).astype(jnp.int16)


def make_image(pieces, probes):
    _, width, cells = pieces.shape
    return pl.pallas_call(
        image_kernel,
        in_specs=[in_vmem(), pl.BlockSpec(memory_space=pltpu.HBM)],
        out_specs=[in_vmem()] * 2,
        out_shape=(
            jax.ShapeDtypeStruct((cells, width), F32),
            jax.ShapeDtypeStruct((cells + TAIL, width), jnp.int16),
        ),
        scratch_shapes=[pltpu.VMEM((cells, width), BF16), pltpu.SemaphoreType.DMA],
        compiler_params=params(4),
        name="make_image",
    )(pieces, probes)


def gram_kernel(image, gram):
    gram[...] = exact_dot(image[...], image[...], ((0,), (0,)))


def make_gram(image):
    width = image.shape[1]
    return pl.pallas_call(
        gram_kernel,
        in_specs=[in_vmem()],
        out_specs=in_vmem(),
        out_shape=jax.ShapeDtypeStruct((width, width), F32),
        compiler_params=params(8),
        name="make_gram",
    )(image)


def spread(pieces, out):
    total = pieces[0]
    for k in range(1, pieces.shape[0]):
        total = total + pieces[k]
    for k in range(out.shape[0]):
        out[k] = total


def spread_sum_kernel(pieces, out):
    spread(pieces, out)


def spread_sum(pieces, copies):
    return pl.pallas_call(
        spread_sum_kernel,
        in_specs=[in_vmem()],
        out_specs=in_vmem(),
        out_shape=jax.ShapeDtypeStruct((copies,) + pieces.shape[1:], F32),
        compiler_params=params(4),
        name="spread_sum",
    )(pieces)


def eliminate(tiles, lane0):
    count, wide = len(tiles), len(tiles[0])
    sub = lax.broadcasted_iota(jnp.int32, (8, 128), 0)
    out = []
    for j in range(count):
        head = tiles[j]

        def columns(tile):
            first = lane0 + 8 * j
            return [
                jnp.broadcast_to(tile[0][:, first + k : first + k + 1], (8, 128)) for k in range(8)
            ]

        cols = columns(head)
        s = [[jnp.broadcast_to(cols[k][i : i + 1, :], (8, 128)) for k in range(i + 1)] for i in range(8)]
        low = [[None] * 8 for _ in range(8)]
        inv = [None] * 8
        for k in range(8):
            inv[k] = lax.rsqrt(s[k][k])
            for i in range(k + 1, 8):
                low[i][k] = s[i][k] * inv[k]
            for i in range(k + 1, 8):
                for m in range(k + 1, i + 1):
                    s[i][m] = s[i][m] - low[i][k] * low[m][k]
        u = []
        for i in range(8):
            parts = []
            for v in range(wide):
                a = jnp.broadcast_to(head[v][i : i + 1, :], (8, 128))
                for k in range(i):
                    a = a - low[i][k] * u[k][v]
                parts.append(a * inv[i])
            u.append(parts)
        rows = []
        for v in range(wide):
            t = u[0][v]
            for i in range(1, 8):
                t = jnp.where(sub == i, u[i][v], t)
            rows.append(t)
        out.append(rows)
        for r in range(j + 1, count):
            c = columns(tiles[r])
            l = []
            for i in range(8):
                a = c[i]
                for k in range(i):
                    a = a - low[i][k] * l[k]
                l.append(a * inv[i])
            new = []
            for v in range(wide):
                t = tiles[r][v]
                for i in range(8):
                    t = t - l[i] * u[i][v]
                new.append(t)
            tiles[r] = new
    return out


def factor_kernel(scale, gram, upper, high, low, work, inverse):
    n = gram.shape[0]
    panels = n // PANEL
    lane = lax.broadcasted_iota(jnp.int32, (8, 128), 1)
    sub = lax.broadcasted_iota(jnp.int32, (8, 128), 0)
    src = gram
    for p in range(panels):
        r0 = p * PANEL
        first, lane0 = r0 // 128, r0 % 128
        used = range(first, n // 128)
        tiles = []
        for t in range(PANEL // 8):
            row = src[r0 + 8 * t : r0 + 8 * t + 8, :]
            unit = jnp.where(lane == sub + 8 * t, 1.0, 0.0).astype(F32)
            tiles.append([row[:, 128 * v : 128 * v + 128] for v in used] + [unit])
        out = eliminate(tiles, lane0)
        rows = [jnp.concatenate([o[v] for o in out], axis=0) for v in range(len(used))]
        corner = jnp.concatenate([o[-1] for o in out], axis=0)[:, :PANEL]
        rows = [jnp.zeros((PANEL, 128), F32)] * first + rows
        u = jnp.concatenate(rows, axis=1)
        row_id = lax.broadcasted_iota(jnp.int32, (PANEL, n), 0) + r0
        col_id = lax.broadcasted_iota(jnp.int32, (PANEL, n), 1)
        u = jnp.where(col_id >= row_id, u, 0.0)
        work[r0 : r0 + PANEL, :] = u
        upper[r0 : r0 + PANEL, :] = u * (1.0 / scale)
        for q0 in range(r0 + PANEL, n, PANEL):
            update = exact_dot(u[:, q0 : q0 + PANEL], u, ((0,), (0,)))
            work[q0 : q0 + PANEL, :] = src[q0 : q0 + PANEL, :] - update
        src = work
        right = jnp.where(col_id == row_id, 1.0, 0.0).astype(F32)
        if p:
            right = right - exact_dot(work[0:r0, r0 : r0 + PANEL], inverse[0:r0, :], ((0,), (0,)))
        inverse[r0 : r0 + PANEL, :] = exact_dot(corner, right, ((1,), (0,)))
    turned = inverse[...].T * scale
    high[...] = turned.astype(BF16)
    low[...] = (turned - high[...].astype(F32)).astype(BF16)


def cholesky_and_inverse(gram, scale):
    n = gram.shape[0]
    full, half = (jax.ShapeDtypeStruct((n, n), t) for t in (F32, BF16))
    return pl.pallas_call(
        functools.partial(factor_kernel, scale),
        in_specs=[in_vmem()],
        out_specs=[in_vmem()] * 3,
        out_shape=(full, half, half),
        scratch_shapes=[pltpu.VMEM((n, n), F32)] * 2,
        compiler_params=params(8),
        name="cholesky_and_inverse",
    )(gram)


def basis_kernel(*refs):
    parts, (high, low, out, staged, sems) = refs[:4], refs[4:]
    rows, width = staged.shape[2:]
    here = position()
    dot = functools.partial(jnp.dot, preferred_element_type=F32)
    copies = []
    for g, part in enumerate(parts):
        pieces = []
        for i in range(4):
            power = part[i, rows:].astype(jnp.int32).astype(F32)[:1]
            piece = part[i, :rows].astype(jnp.int32).astype(F32)
            pieces.append(piece * (jnp.exp2(power) * (1.0 / CODE_TOP)))
        x = jnp.concatenate(pieces, axis=0)
        x_high = x.astype(BF16)
        x_low = (x - x_high.astype(F32)).astype(BF16)
        y = dot(x_high, high[...]) + (dot(x_high, low[...]) + dot(x_low, high[...]))
        staged[g] = y.reshape(4, rows, width)
        for i in range(4):
            source = 4 * i + ((here % 4) ^ g)
            to = pl.ds(pl.multiple_of(source * rows, rows), rows)
            copy = pltpu.make_async_copy(staged.at[g, i], out.at[to], sems.at[4 * g + i])
            copy.start()
            copies.append(copy)
    for copy in copies:
        copy.wait()


def make_basis(parts, high, low):
    count, rows, width = parts[0].shape
    rows -= TAIL
    return pl.pallas_call(
        basis_kernel,
        in_specs=[in_vmem()] * 6,
        out_specs=pl.BlockSpec(memory_space=pltpu.HBM),
        out_shape=jax.ShapeDtypeStruct((4 * count * rows, width), F32),
        scratch_shapes=[
            pltpu.VMEM((4, count, rows, width), F32),
            pltpu.SemaphoreType.DMA((4 * count,)),
        ],
        compiler_params=params(16),
        name="make_basis",
    )(*parts, high, low)


def paired(value, axis, first):
    pairs = [(i, i + 1) for i in range(first, lax.axis_size(axis) - 1, 2)]
    return lax.ppermute(value, axis, pairs + [(j, i) for i, j in pairs])


def body(probes, weights, columns):
    rows, width = probes.shape
    w_local = weights[0]
    blocks, _, bs, _ = w_local.shape
    far = paired(probes, "brick", 1)
    near = paired(probes, "brick", 0)
    shape = (blocks, bs, width)
    cols = columns.reshape(-1)
    w_sorted, own_data = start_operator(cols, w_local, probes.reshape(shape))
    own, *to_far, to_near = finish_operator(cols, w_sorted, own_data, far.reshape(shape), near.reshape(shape))

    n = lax.axis_size(DEPTH)

    def swap(held, distance):
        return lax.ppermute(held, DEPTH, [(i, i ^ distance) for i in range(n)])

    from_far = [paired(to_far[0], "brick", 1), paired(to_far[1], "brick", 1)]
    from_near = paired(to_near, "brick", 0)
    halves = []
    for k, part in enumerate(from_far):
        keep, send = split_parity(k * part.shape[0], own, part, from_near)
        halves += [keep, swap(send, 1)]
    held = add_pair(*halves)
    image, coded = make_image(lax.all_to_all(held, ("za", "zb"), 0, 0), probes)

    held = lax.all_gather(coded, "za")
    gram = make_gram(image)
    bricks = lax.axis_size("brick")
    share = lax.all_to_all(gram.reshape(bricks, width // bricks, width), "brick", 0, 0)
    share = lax.all_to_all(spread_sum(share, n), DEPTH, 0, 0)
    parts = [held] + [swap(held, k) for k in (1, 2, 3)]
    gram = lax.all_to_all(spread_sum(share, bricks), "brick", 0, 0).reshape(width, width)

    scale = math.sqrt(rows * bricks)
    upper, high, low = cholesky_and_inverse(gram, scale)
    return make_basis(parts, high, low), upper


def solution(mesh):
    deep = mesh.devices.reshape(mesh.devices.shape[0] // 4, 2, 2, mesh.devices.shape[1])
    mesh = Mesh(deep, DEPTH + ("brick",))
    in_specs = (P("brick", None), P(DEPTH, "brick", None, None, None), P(DEPTH, "brick", None))
    out_specs = (P("brick", None), P())
    return jax.shard_map(body, mesh=mesh, in_specs=in_specs, out_specs=out_specs, check_vma=False)
```

```python
import functools
import math

import jax
import jax.numpy as jnp
from jax import lax
from jax.experimental import pallas as pl
from jax.experimental.pallas import tpu as pltpu
from jax.sharding import Mesh
from jax.sharding import PartitionSpec as P

F32 = jnp.float32
BF16 = jnp.bfloat16
PANEL = 64
MIB = 1024 * 1024
DEPTH = ("za", "zb", "zc")
TAIL = 16
CODE_TOP = 32000.0


def position():
    return 4 * lax.axis_index("za") + 2 * lax.axis_index("zb") + lax.axis_index("zc")


def exact_dot(a, b, dims):
    return lax.dot_general(
        a, b, (dims, ((), ())), precision=lax.Precision.HIGHEST, preferred_element_type=F32
    )


def in_vmem():
    return pl.BlockSpec(memory_space=pltpu.VMEM)


def params(mib):
    return pltpu.CompilerParams(vmem_limit_bytes=mib * MIB)


def places(cols, r, blocks):
    ids = [cols[3 * r + j] for j in range(3)]
    at_low = jnp.where(ids[0] < blocks, 0, jnp.where(ids[1] < blocks, 1, 2))
    at_high = jnp.where(ids[0] >= 2 * blocks, 0, jnp.where(ids[1] >= 2 * blocks, 1, 2))
    at_own = 3 - at_low - at_high
    low, high = cols[3 * r + at_low], cols[3 * r + at_high] - 2 * blocks
    first = lax.axis_index("brick") % 2 == 0
    at = (jnp.where(first, at_low, at_high), at_own, jnp.where(first, at_high, at_low))
    return at, jnp.where(first, low, high), jnp.where(first, high, low)


def own_kernel(cols, w_ref, own_ref, w_out, data_out):
    blocks = own_ref.shape[0]

    def step(r, carry):
        at, _, _ = places(cols, r, blocks)
        for j in range(3):
            w_out[r, j] = w_ref[r, at[j]]
        data_out[r] = jnp.dot(w_ref[r, at[1]], own_ref[r], preferred_element_type=F32)
        return carry

    lax.fori_loop(0, blocks, step, 0)


def start_operator(cols, weights, own):
    blocks, slots, bs, _ = weights.shape
    width = own.shape[-1]
    return pl.pallas_call(
        own_kernel,
        in_specs=[pl.BlockSpec(memory_space=pltpu.SMEM), in_vmem(), in_vmem()],
        out_specs=[in_vmem()] * 2,
        out_shape=(
            jax.ShapeDtypeStruct(weights.shape, BF16),
            jax.ShapeDtypeStruct((blocks, bs, width), F32),
        ),
        compiler_params=params(14),
        cost_estimate=pl.CostEstimate(
            flops=2 * blocks * bs * bs * width, bytes_accessed=9 * MIB, transcendentals=0
        ),
        name="own_data",
    )(cols, weights, own)


def operator_kernel(
    cols, w_ref, data_ref, far_ref, near_ref, own_out, far_first, far_last, near_first, near_last, s_far, s_near, d_ref
):
    blocks, _, bs, _ = w_ref.shape
    dot = functools.partial(jnp.dot, preferred_element_type=F32)
    s_far[...] = jnp.zeros_like(s_far)
    s_near[...] = jnp.zeros_like(s_near)

    def data_of(r):
        _, far, near = places(cols, r, blocks)
        w = jnp.concatenate([w_ref[r, 0], w_ref[r, 2]], axis=1)
        probes = jnp.concatenate([far_ref[far], near_ref[near]], axis=0)
        return (data_ref[r] + dot(w, probes)).astype(BF16).T

    def put(r):
        _, far, near = places(cols, r, blocks)
        w = jnp.concatenate([w_ref[r, j] for j in range(3)], axis=1)
        terms = dot(d_ref[r % 2], w)
        own_out[2 * r] = terms[:, bs : bs + 128]
        own_out[2 * r + 1] = terms[:, bs + 128 : 2 * bs]
        s_far[far] += terms[:, :bs]
        s_near[near] += terms[:, 2 * bs :]

    d_ref[0] = data_of(0)

    def step(r, carry):
        later = data_of(r + 1)
        put(r)
        d_ref[(r + 1) % 2] = later
        return carry

    lax.fori_loop(0, blocks - 1, step, 0)
    put(blocks - 1)
    half = blocks // 2
    for q in range(blocks):
        outs = (far_first, near_first) if q < half else (far_last, near_last)
        for out, field in zip(outs, (s_far, s_near)):
            k = q % half
            out[2 * k] = field[q, :, :128].astype(BF16)
            out[2 * k + 1] = field[q, :, 128:].astype(BF16)


def finish_operator(cols, weights, data, far, near):
    blocks, _, bs, _ = weights.shape
    width = data.shape[-1]
    shape = (2 * blocks, width, bs // 2)
    half = jax.ShapeDtypeStruct((blocks, width, bs // 2), BF16)
    field = pltpu.VMEM((blocks, width, bs), F32)
    return pl.pallas_call(
        operator_kernel,
        in_specs=[pl.BlockSpec(memory_space=pltpu.SMEM)] + [in_vmem()] * 4,
        out_specs=[in_vmem()] * 5,
        out_shape=(
            jax.ShapeDtypeStruct(shape, F32),
            half,
            half,
            half,
            half,
        ),
        scratch_shapes=[field, field, pltpu.VMEM((2, width, bs), BF16)],
        compiler_params=params(20),
        name="normal_operator",
    )(cols, weights, data, far, near)


def parity_kernel(first, own, far, near, keep, send):
    odd = lax.axis_index("zc")
    for out, parity in ((keep, odd), (send, 1 - odd)):
        for i in range(out.shape[0]):
            p = 2 * i + parity
            total = far[p].astype(F32) + near[p].astype(F32)
            out[i] = (own[first + p] + total).astype(out.dtype)


def split_parity(first, own, far, near):
    pieces, width, cells = far.shape
    kept, sent = (jax.ShapeDtypeStruct((pieces // 2, width, cells), t) for t in (F32, BF16))
    return pl.pallas_call(
        functools.partial(parity_kernel, first),
        in_specs=[in_vmem()] * 3,
        out_specs=[in_vmem()] * 2,
        out_shape=(kept, sent),
        compiler_params=params(12),
        name="split_parity",
    )(own, far, near)


def pair_kernel(keep, got, keep_last, got_last, out):
    n = keep.shape[0]
    for i in range(n):
        out[i] = (keep[i] + got[i].astype(F32)).astype(BF16)
        out[n + i] = (keep_last[i] + got_last[i].astype(F32)).astype(BF16)


def add_pair(*halves):
    n, width, cells = halves[0].shape
    return pl.pallas_call(
        pair_kernel,
        in_specs=[in_vmem()] * 4,
        out_specs=in_vmem(),
        out_shape=jax.ShapeDtypeStruct((2 * n, width, cells), BF16),
        compiler_params=params(8),
        name="add_pair",
    )(*halves)


def image_kernel(pieces, probes, image, coded, own, sem):
    rows = own.shape[0]
    block = position()
    copy = pltpu.make_async_copy(probes.at[pl.ds(block * rows, rows)], own, sem)
    copy.start()
    total = pieces[0].astype(F32)
    for k in range(1, pieces.shape[0]):
        total = total + pieces[k].astype(F32)
    copy.wait()
    x = own[...].astype(F32) + total.T
    image[...] = x
    top = jnp.maximum(jnp.max(jnp.abs(x), axis=0, keepdims=True), 1e-30)
    power = jnp.ceil(jnp.log(top) * (1.0 / math.log(2.0)))
    whole = jnp.floor(x * (jnp.exp2(-power) * CODE_TOP) + 0.5)
    coded[:rows] = whole.astype(jnp.int32).astype(jnp.int16)
    tail = jnp.broadcast_to(power, (TAIL, x.shape[1]))
    coded[rows:] = tail.astype(jnp.int32).astype(jnp.int16)


def make_image(pieces, probes):
    _, width, cells = pieces.shape
    return pl.pallas_call(
        image_kernel,
        in_specs=[in_vmem(), pl.BlockSpec(memory_space=pltpu.HBM)],
        out_specs=[in_vmem()] * 2,
        out_shape=(
            jax.ShapeDtypeStruct((cells, width), F32),
            jax.ShapeDtypeStruct((cells + TAIL, width), jnp.int16),
        ),
        scratch_shapes=[pltpu.VMEM((cells, width), BF16), pltpu.SemaphoreType.DMA],
        compiler_params=params(4),
        name="make_image",
    )(pieces, probes)


def gram_kernel(image, gram):
    gram[...] = exact_dot(image[...], image[...], ((0,), (0,)))


def make_gram(image):
    width = image.shape[1]
    return pl.pallas_call(
        gram_kernel,
        in_specs=[in_vmem()],
        out_specs=in_vmem(),
        out_shape=jax.ShapeDtypeStruct((width, width), F32),
        compiler_params=params(8),
        name="make_gram",
    )(image)


def spread(pieces, out):
    total = pieces[0]
    for k in range(1, pieces.shape[0]):
        total = total + pieces[k]
    for k in range(out.shape[0]):
        out[k] = total


def spread_sum_kernel(pieces, out):
    spread(pieces, out)


def spread_sum(pieces, copies):
    return pl.pallas_call(
        spread_sum_kernel,
        in_specs=[in_vmem()],
        out_specs=in_vmem(),
        out_shape=jax.ShapeDtypeStruct((copies,) + pieces.shape[1:], F32),
        compiler_params=params(4),
        name="spread_sum",
    )(pieces)


def eliminate(tiles, lane0):
    count, wide = len(tiles), len(tiles[0])
    sub = lax.broadcasted_iota(jnp.int32, (8, 128), 0)
    out = []
    for j in range(count):
        head = tiles[j]

        def columns(tile):
            first = lane0 + 8 * j
            return [
                jnp.broadcast_to(tile[0][:, first + k : first + k + 1], (8, 128)) for k in range(8)
            ]

        cols = columns(head)
        s = [[jnp.broadcast_to(cols[k][i : i + 1, :], (8, 128)) for k in range(i + 1)] for i in range(8)]
        low = [[None] * 8 for _ in range(8)]
        inv = [None] * 8
        for k in range(8):
            inv[k] = lax.rsqrt(s[k][k])
            for i in range(k + 1, 8):
                low[i][k] = s[i][k] * inv[k]
            for i in range(k + 1, 8):
                for m in range(k + 1, i + 1):
                    s[i][m] = s[i][m] - low[i][k] * low[m][k]
        u = []
        for i in range(8):
            parts = []
            for v in range(wide):
                a = jnp.broadcast_to(head[v][i : i + 1, :], (8, 128))
                for k in range(i):
                    a = a - low[i][k] * u[k][v]
                parts.append(a * inv[i])
            u.append(parts)
        rows = []
        for v in range(wide):
            t = u[0][v]
            for i in range(1, 8):
                t = jnp.where(sub == i, u[i][v], t)
            rows.append(t)
        out.append(rows)
        for r in range(j + 1, count):
            c = columns(tiles[r])
            l = []
            for i in range(8):
                a = c[i]
                for k in range(i):
                    a = a - low[i][k] * l[k]
                l.append(a * inv[i])
            new = []
            for v in range(wide):
                t = tiles[r][v]
                for i in range(8):
                    t = t - l[i] * u[i][v]
                new.append(t)
            tiles[r] = new
    return out


def factor_kernel(scale, gram, upper, high, low, work, inverse):
    n = gram.shape[0]
    panels = n // PANEL
    lane = lax.broadcasted_iota(jnp.int32, (8, 128), 1)
    sub = lax.broadcasted_iota(jnp.int32, (8, 128), 0)
    src = gram
    for p in range(panels):
        r0 = p * PANEL
        first, lane0 = r0 // 128, r0 % 128
        used = range(first, n // 128)
        tiles = []
        for t in range(PANEL // 8):
            row = src[r0 + 8 * t : r0 + 8 * t + 8, :]
            unit = jnp.where(lane == sub + 8 * t, 1.0, 0.0).astype(F32)
            tiles.append([row[:, 128 * v : 128 * v + 128] for v in used] + [unit])
        out = eliminate(tiles, lane0)
        rows = [jnp.concatenate([o[v] for o in out], axis=0) for v in range(len(used))]
        corner = jnp.concatenate([o[-1] for o in out], axis=0)[:, :PANEL]
        rows = [jnp.zeros((PANEL, 128), F32)] * first + rows
        u = jnp.concatenate(rows, axis=1)
        row_id = lax.broadcasted_iota(jnp.int32, (PANEL, n), 0) + r0
        col_id = lax.broadcasted_iota(jnp.int32, (PANEL, n), 1)
        u = jnp.where(col_id >= row_id, u, 0.0)
        work[r0 : r0 + PANEL, :] = u
        upper[r0 : r0 + PANEL, :] = u * (1.0 / scale)
        for q0 in range(r0 + PANEL, n, PANEL):
            update = exact_dot(u[:, q0 : q0 + PANEL], u, ((0,), (0,)))
            work[q0 : q0 + PANEL, :] = src[q0 : q0 + PANEL, :] - update
        src = work
        right = jnp.where(col_id == row_id, 1.0, 0.0).astype(F32)
        if p:
            right = right - exact_dot(work[0:r0, r0 : r0 + PANEL], inverse[0:r0, :], ((0,), (0,)))
        inverse[r0 : r0 + PANEL, :] = exact_dot(corner, right, ((1,), (0,)))
    turned = inverse[...].T * scale
    high[...] = turned.astype(BF16)
    low[...] = (turned - high[...].astype(F32)).astype(BF16)


def cholesky_and_inverse(gram, scale):
    n = gram.shape[0]
    full, half = (jax.ShapeDtypeStruct((n, n), t) for t in (F32, BF16))
    return pl.pallas_call(
        functools.partial(factor_kernel, scale),
        in_specs=[in_vmem()],
        out_specs=[in_vmem()] * 3,
        out_shape=(full, half, half),
        scratch_shapes=[pltpu.VMEM((n, n), F32)] * 2,
        compiler_params=params(8),
        name="cholesky_and_inverse",
    )(gram)


def basis_kernel(*refs):
    parts, (high, low, out, staged, sems) = refs[:4], refs[4:]
    rows, width = staged.shape[2:]
    here = position()
    dot = functools.partial(jnp.dot, preferred_element_type=F32)
    copies = []
    for g, part in enumerate(parts):
        pieces = []
        for i in range(4):
            power = part[i, rows:].astype(jnp.int32).astype(F32)[:1]
            piece = part[i, :rows].astype(jnp.int32).astype(F32)
            pieces.append(piece * (jnp.exp2(power) * (1.0 / CODE_TOP)))
        x = jnp.concatenate(pieces, axis=0)
        x_high = x.astype(BF16)
        x_low = (x - x_high.astype(F32)).astype(BF16)
        y = dot(x_high, high[...]) + (dot(x_high, low[...]) + dot(x_low, high[...]))
        staged[g] = y.reshape(4, rows, width)
        for i in range(4):
            source = 4 * i + ((here % 4) ^ g)
            to = pl.ds(pl.multiple_of(source * rows, rows), rows)
            copy = pltpu.make_async_copy(staged.at[g, i], out.at[to], sems.at[4 * g + i])
            copy.start()
            copies.append(copy)
    for copy in copies:
        copy.wait()


def make_basis(parts, high, low):
    count, rows, width = parts[0].shape
    rows -= TAIL
    return pl.pallas_call(
        basis_kernel,
        in_specs=[in_vmem()] * 6,
        out_specs=pl.BlockSpec(memory_space=pltpu.HBM),
        out_shape=jax.ShapeDtypeStruct((4 * count * rows, width), F32),
        scratch_shapes=[
            pltpu.VMEM((4, count, rows, width), F32),
            pltpu.SemaphoreType.DMA((4 * count,)),
        ],
        compiler_params=params(16),
        name="make_basis",
    )(*parts, high, low)


def paired(value, axis, first):
    pairs = [(i, i + 1) for i in range(first, lax.axis_size(axis) - 1, 2)]
    return lax.ppermute(value, axis, pairs + [(j, i) for i, j in pairs])


def body(probes, weights, columns):
    rows, width = probes.shape
    w_local = weights[0]
    blocks, _, bs, _ = w_local.shape
    far = paired(probes, "brick", 1)
    near = paired(probes, "brick", 0)
    shape = (blocks, bs, width)
    cols = columns.reshape(-1)
    w_sorted, own_data = start_operator(cols, w_local, probes.reshape(shape))
    own, *sent = finish_operator(cols, w_sorted, own_data, far.reshape(shape), near.reshape(shape))

    n = lax.axis_size(DEPTH)

    def swap(held, distance):
        return lax.ppermute(held, DEPTH, [(i, i ^ distance) for i in range(n)])

    from_far = [paired(part, "brick", 1) for part in sent[:2]]
    from_near = [paired(part, "brick", 0) for part in sent[2:]]
    halves = []
    for k, part in enumerate(from_far):
        keep, send = split_parity(k * part.shape[0], own, part, from_near[k])
        halves += [keep, swap(send, 1)]
    held = add_pair(*halves)
    image, coded = make_image(lax.all_to_all(held, ("za", "zb"), 0, 0), probes)

    held = lax.all_gather(coded, "za")
    gram = make_gram(image)
    bricks = lax.axis_size("brick")
    share = lax.all_to_all(gram.reshape(bricks, width // bricks, width), "brick", 0, 0)
    share = lax.all_to_all(spread_sum(share, n), DEPTH, 0, 0)
    parts = [held] + [swap(held, k) for k in (1, 2, 3)]
    gram = lax.all_to_all(spread_sum(share, bricks), "brick", 0, 0).reshape(width, width)

    scale = math.sqrt(rows * bricks)
    upper, high, low = cholesky_and_inverse(gram, scale)
    return make_basis(parts, high, low), upper


def solution(mesh):
    deep = mesh.devices.reshape(mesh.devices.shape[0] // 4, 2, 2, mesh.devices.shape[1])
    mesh = Mesh(deep, DEPTH + ("brick",))
    in_specs = (P("brick", None), P(DEPTH, "brick", None, None, None), P(DEPTH, "brick", None))
    out_specs = (P("brick", None), P())
    return jax.shard_map(body, mesh=mesh, in_specs=in_specs, out_specs=out_specs, check_vma=False)
```

```python
import functools
import math

import jax
import jax.numpy as jnp
from jax import lax
from jax.experimental import pallas as pl
from jax.experimental.pallas import tpu as pltpu
from jax.sharding import Mesh
from jax.sharding import PartitionSpec as P

F32 = jnp.float32
BF16 = jnp.bfloat16
PANEL = 64
MIB = 1024 * 1024
DEPTH = ("za", "zb", "zc")
TAIL = 16
CODE_TOP = 32000.0


def position():
    return 4 * lax.axis_index("za") + 2 * lax.axis_index("zb") + lax.axis_index("zc")


def exact_dot(a, b, dims):
    return lax.dot_general(
        a, b, (dims, ((), ())), precision=lax.Precision.HIGHEST, preferred_element_type=F32
    )


def in_vmem():
    return pl.BlockSpec(memory_space=pltpu.VMEM)


def params(mib):
    return pltpu.CompilerParams(vmem_limit_bytes=mib * MIB)


def places(cols, r, blocks):
    ids = [cols[3 * r + j] for j in range(3)]
    at_low = jnp.where(ids[0] < blocks, 0, jnp.where(ids[1] < blocks, 1, 2))
    at_high = jnp.where(ids[0] >= 2 * blocks, 0, jnp.where(ids[1] >= 2 * blocks, 1, 2))
    at_own = 3 - at_low - at_high
    low, high = cols[3 * r + at_low], cols[3 * r + at_high] - 2 * blocks
    first = lax.axis_index("brick") % 2 == 0
    at = (jnp.where(first, at_low, at_high), at_own, jnp.where(first, at_high, at_low))
    return at, jnp.where(first, low, high), jnp.where(first, high, low)


def own_kernel(cols, w_ref, own_ref, w_out, data_out):
    blocks = own_ref.shape[0]

    def step(r, carry):
        at, _, _ = places(cols, r, blocks)
        for j in range(3):
            w_out[r, j] = w_ref[r, at[j]]
        data_out[r] = jnp.dot(w_ref[r, at[1]], own_ref[r], preferred_element_type=F32)
        return carry

    lax.fori_loop(0, blocks, step, 0)


def start_operator(cols, weights, own):
    blocks, slots, bs, _ = weights.shape
    width = own.shape[-1]
    return pl.pallas_call(
        own_kernel,
        in_specs=[pl.BlockSpec(memory_space=pltpu.SMEM), in_vmem(), in_vmem()],
        out_specs=[in_vmem()] * 2,
        out_shape=(
            jax.ShapeDtypeStruct(weights.shape, BF16),
            jax.ShapeDtypeStruct((blocks, bs, width), F32),
        ),
        compiler_params=params(14),
        cost_estimate=pl.CostEstimate(
            flops=2 * blocks * bs * bs * width, bytes_accessed=9 * MIB, transcendentals=0
        ),
        name="own_data",
    )(cols, weights, own)


def operator_kernel(
    cols, w_ref, data_ref, far_ref, near_ref, own_out, far_first, far_last, near_first, near_last, s_far, s_near, d_ref
):
    blocks, _, bs, _ = w_ref.shape
    dot = functools.partial(jnp.dot, preferred_element_type=F32)
    s_far[...] = jnp.zeros_like(s_far)
    s_near[...] = jnp.zeros_like(s_near)

    def data_of(r):
        _, far, near = places(cols, r, blocks)
        w = jnp.concatenate([w_ref[r, 0], w_ref[r, 2]], axis=1)
        probes = jnp.concatenate([far_ref[far], near_ref[near]], axis=0)
        return (data_ref[r] + dot(w, probes)).astype(BF16).T

    def put(r):
        _, far, near = places(cols, r, blocks)
        w = jnp.concatenate([w_ref[r, j] for j in range(3)], axis=1)
        terms = dot(d_ref[r % 2], w)
        own_out[2 * r] = terms[:, bs : bs + 128]
        own_out[2 * r + 1] = terms[:, bs + 128 : 2 * bs]
        s_far[far] += terms[:, :bs]
        s_near[near] += terms[:, 2 * bs :]

    d_ref[0] = data_of(0)

    def step(r, carry):
        later = data_of(r + 1)
        put(r)
        d_ref[(r + 1) % 2] = later
        return carry

    lax.fori_loop(0, blocks - 1, step, 0)
    put(blocks - 1)
    half = blocks // 2
    for q in range(blocks):
        outs = (far_first, near_first) if q < half else (far_last, near_last)
        for out, field in zip(outs, (s_far, s_near)):
            k = q % half
            out[2 * k] = field[q, :, :128].astype(BF16)
            out[2 * k + 1] = field[q, :, 128:].astype(BF16)


def finish_operator(cols, weights, data, far, near):
    blocks, _, bs, _ = weights.shape
    width = data.shape[-1]
    shape = (2 * blocks, width, bs // 2)
    half = jax.ShapeDtypeStruct((blocks, width, bs // 2), BF16)
    field = pltpu.VMEM((blocks, width, bs), F32)
    return pl.pallas_call(
        operator_kernel,
        in_specs=[pl.BlockSpec(memory_space=pltpu.SMEM)] + [in_vmem()] * 4,
        out_specs=[in_vmem()] * 5,
        out_shape=(
            jax.ShapeDtypeStruct(shape, F32),
            half,
            half,
            half,
            half,
        ),
        scratch_shapes=[field, field, pltpu.VMEM((2, width, bs), BF16)],
        compiler_params=params(20),
        name="normal_operator",
    )(cols, weights, data, far, near)


def parity_kernel(first, own, far, near, keep, send):
    odd = lax.axis_index("zc")
    for out, parity in ((keep, odd), (send, 1 - odd)):
        for i in range(out.shape[0]):
            p = 2 * i + parity
            total = far[p].astype(F32) + near[p].astype(F32)
            out[i] = (own[first + p] + total).astype(out.dtype)


def split_parity(first, own, far, near):
    pieces, width, cells = far.shape
    kept, sent = (jax.ShapeDtypeStruct((pieces // 2, width, cells), t) for t in (F32, BF16))
    return pl.pallas_call(
        functools.partial(parity_kernel, first),
        in_specs=[in_vmem()] * 3,
        out_specs=[in_vmem()] * 2,
        out_shape=(kept, sent),
        compiler_params=params(12),
        name="split_parity",
    )(own, far, near)


def pair_kernel(keep, got, keep_last, got_last, out):
    n = keep.shape[0]
    for i in range(n):
        out[i] = (keep[i] + got[i].astype(F32)).astype(BF16)
        out[n + i] = (keep_last[i] + got_last[i].astype(F32)).astype(BF16)


def add_pair(*halves):
    n, width, cells = halves[0].shape
    return pl.pallas_call(
        pair_kernel,
        in_specs=[in_vmem()] * 4,
        out_specs=in_vmem(),
        out_shape=jax.ShapeDtypeStruct((2 * n, width, cells), BF16),
        compiler_params=params(8),
        name="add_pair",
    )(*halves)


def image_kernel(pieces, probes, image, coded, own, sem):
    rows = own.shape[0]
    block = position()
    copy = pltpu.make_async_copy(probes.at[pl.ds(block * rows, rows)], own, sem)
    copy.start()
    total = pieces[0].astype(F32)
    for k in range(1, pieces.shape[0]):
        total = total + pieces[k].astype(F32)
    copy.wait()
    x = own[...].astype(F32) + total.T
    image[...] = x
    top = jnp.maximum(jnp.max(jnp.abs(x), axis=0, keepdims=True), 1e-30)
    power = jnp.ceil(jnp.log(top) * (1.0 / math.log(2.0)))
    whole = jnp.floor(x * (jnp.exp2(-power) * CODE_TOP) + 0.5)
    coded[:rows] = whole.astype(jnp.int32).astype(jnp.int16)
    tail = jnp.broadcast_to(power, (TAIL, x.shape[1]))
    coded[rows:] = tail.astype(jnp.int32).astype(jnp.int16)


def make_image(pieces, probes):
    _, width, cells = pieces.shape
    return pl.pallas_call(
        image_kernel,
        in_specs=[in_vmem(), pl.BlockSpec(memory_space=pltpu.HBM)],
        out_specs=[in_vmem()] * 2,
        out_shape=(
            jax.ShapeDtypeStruct((cells, width), F32),
            jax.ShapeDtypeStruct((cells + TAIL, width), jnp.int16),
        ),
        scratch_shapes=[pltpu.VMEM((cells, width), BF16), pltpu.SemaphoreType.DMA],
        compiler_params=params(4),
        name="make_image",
    )(pieces, probes)


def gram_kernel(image, gram):
    gram[...] = exact_dot(image[...], image[...], ((0,), (0,)))


def make_gram(image):
    width = image.shape[1]
    return pl.pallas_call(
        gram_kernel,
        in_specs=[in_vmem()],
        out_specs=in_vmem(),
        out_shape=jax.ShapeDtypeStruct((width, width), F32),
        compiler_params=params(8),
        name="make_gram",
    )(image)


def spread(pieces, out):
    total = pieces[0]
    for k in range(1, pieces.shape[0]):
        total = total + pieces[k]
    for k in range(out.shape[0]):
        out[k] = total


def spread_sum_kernel(pieces, out):
    spread(pieces, out)


def spread_sum(pieces, copies):
    return pl.pallas_call(
        spread_sum_kernel,
        in_specs=[in_vmem()],
        out_specs=in_vmem(),
        out_shape=jax.ShapeDtypeStruct((copies,) + pieces.shape[1:], F32),
        compiler_params=params(4),
        name="spread_sum",
    )(pieces)


def eliminate(tiles, lane0):
    count, wide = len(tiles), len(tiles[0])
    sub = lax.broadcasted_iota(jnp.int32, (8, 128), 0)
    out = []
    for j in range(count):
        head = tiles[j]

        def columns(tile):
            first = lane0 + 8 * j
            return [
                jnp.broadcast_to(tile[0][:, first + k : first + k + 1], (8, 128)) for k in range(8)
            ]

        cols = columns(head)
        s = [[jnp.broadcast_to(cols[k][i : i + 1, :], (8, 128)) for k in range(i + 1)] for i in range(8)]
        low = [[None] * 8 for _ in range(8)]
        inv = [None] * 8
        for k in range(8):
            inv[k] = lax.rsqrt(s[k][k])
            for i in range(k + 1, 8):
                low[i][k] = s[i][k] * inv[k]
            for i in range(k + 1, 8):
                for m in range(k + 1, i + 1):
                    s[i][m] = s[i][m] - low[i][k] * low[m][k]
        u = []
        for i in range(8):
            parts = []
            for v in range(wide):
                a = jnp.broadcast_to(head[v][i : i + 1, :], (8, 128))
                for k in range(i):
                    a = a - low[i][k] * u[k][v]
                parts.append(a * inv[i])
            u.append(parts)
        rows = []
        for v in range(wide):
            t = u[0][v]
            for i in range(1, 8):
                t = jnp.where(sub == i, u[i][v], t)
            rows.append(t)
        out.append(rows)
        for r in range(j + 1, count):
            c = columns(tiles[r])
            l = []
            for i in range(8):
                a = c[i]
                for k in range(i):
                    a = a - low[i][k] * l[k]
                l.append(a * inv[i])
            new = []
            for v in range(wide):
                t = tiles[r][v]
                for i in range(8):
                    t = t - l[i] * u[i][v]
                new.append(t)
            tiles[r] = new
    return out


def factor_kernel(scale, gram, upper, high, low, work, inverse):
    n = gram.shape[0]
    panels = n // PANEL
    lane = lax.broadcasted_iota(jnp.int32, (8, 128), 1)
    sub = lax.broadcasted_iota(jnp.int32, (8, 128), 0)
    src = gram
    for p in range(panels):
        r0 = p * PANEL
        first, lane0 = r0 // 128, r0 % 128
        used = range(first, n // 128)
        tiles = []
        for t in range(PANEL // 8):
            row = src[r0 + 8 * t : r0 + 8 * t + 8, :]
            unit = jnp.where(lane == sub + 8 * t, 1.0, 0.0).astype(F32)
            tiles.append([row[:, 128 * v : 128 * v + 128] for v in used] + [unit])
        out = eliminate(tiles, lane0)
        rows = [jnp.concatenate([o[v] for o in out], axis=0) for v in range(len(used))]
        corner = jnp.concatenate([o[-1] for o in out], axis=0)[:, :PANEL]
        rows = [jnp.zeros((PANEL, 128), F32)] * first + rows
        u = jnp.concatenate(rows, axis=1)
        row_id = lax.broadcasted_iota(jnp.int32, (PANEL, n), 0) + r0
        col_id = lax.broadcasted_iota(jnp.int32, (PANEL, n), 1)
        u = jnp.where(col_id >= row_id, u, 0.0)
        work[r0 : r0 + PANEL, :] = u
        upper[r0 : r0 + PANEL, :] = u * (1.0 / scale)
        for q0 in range(r0 + PANEL, n, PANEL):
            update = exact_dot(u[:, q0 : q0 + PANEL], u, ((0,), (0,)))
            work[q0 : q0 + PANEL, :] = src[q0 : q0 + PANEL, :] - update
        src = work
        right = jnp.where(col_id == row_id, 1.0, 0.0).astype(F32)
        if p:
            right = right - exact_dot(work[0:r0, r0 : r0 + PANEL], inverse[0:r0, :], ((0,), (0,)))
        inverse[r0 : r0 + PANEL, :] = exact_dot(corner, right, ((1,), (0,)))
    turned = inverse[...].T * scale
    high[...] = turned.astype(BF16)
    low[...] = (turned - high[...].astype(F32)).astype(BF16)


def cholesky_and_inverse(gram, scale):
    n = gram.shape[0]
    full, half = (jax.ShapeDtypeStruct((n, n), t) for t in (F32, BF16))
    return pl.pallas_call(
        functools.partial(factor_kernel, scale),
        in_specs=[in_vmem()],
        out_specs=[in_vmem()] * 3,
        out_shape=(full, half, half),
        scratch_shapes=[pltpu.VMEM((n, n), F32)] * 2,
        compiler_params=params(8),
        name="cholesky_and_inverse",
    )(gram)


def basis_kernel(*refs):
    parts, (high, low, out, staged, sems) = refs[:4], refs[4:]
    rows, width = staged.shape[2:]
    here = position()
    dot = functools.partial(jnp.dot, preferred_element_type=F32)
    copies = []
    for g, part in enumerate(parts):
        pieces = []
        for i in range(4):
            power = part[i, rows:].astype(jnp.int32).astype(F32)[:1]
            piece = part[i, :rows].astype(jnp.int32).astype(F32)
            pieces.append(piece * (jnp.exp2(power) * (1.0 / CODE_TOP)))
        x = jnp.concatenate(pieces, axis=0)
        x_high = x.astype(BF16)
        x_low = (x - x_high.astype(F32)).astype(BF16)
        y = dot(x_high, high[...]) + (dot(x_high, low[...]) + dot(x_low, high[...]))
        staged[g] = y.reshape(4, rows, width)
        for i in range(4):
            source = 4 * i + ((here % 4) ^ g)
            to = pl.ds(pl.multiple_of(source * rows, rows), rows)
            copy = pltpu.make_async_copy(staged.at[g, i], out.at[to], sems.at[4 * g + i])
            copy.start()
            copies.append(copy)
    for copy in copies:
        copy.wait()


def make_basis(parts, high, low):
    count, rows, width = parts[0].shape
    rows -= TAIL
    return pl.pallas_call(
        basis_kernel,
        in_specs=[in_vmem()] * 6,
        out_specs=pl.BlockSpec(memory_space=pltpu.HBM),
        out_shape=jax.ShapeDtypeStruct((4 * count * rows, width), F32),
        scratch_shapes=[
            pltpu.VMEM((4, count, rows, width), F32),
            pltpu.SemaphoreType.DMA((4 * count,)),
        ],
        compiler_params=params(16),
        name="make_basis",
    )(*parts, high, low)


def paired(value, axis, first):
    pairs = [(i, i + 1) for i in range(first, lax.axis_size(axis) - 1, 2)]
    return lax.ppermute(value, axis, pairs + [(j, i) for i, j in pairs])


def body(probes, weights, columns):
    rows, width = probes.shape
    w_local = weights[0]
    blocks, _, bs, _ = w_local.shape
    far = paired(probes, "brick", 1)
    near = paired(probes, "brick", 0)
    shape = (blocks, bs, width)
    cols = columns.reshape(-1)
    w_sorted, own_data = start_operator(cols, w_local, probes.reshape(shape))
    own, *sent = finish_operator(cols, w_sorted, own_data, far.reshape(shape), near.reshape(shape))

    n = lax.axis_size(DEPTH)

    def swap(held, distance):
        return lax.ppermute(held, DEPTH, [(i, i ^ distance) for i in range(n)])

    from_far = [paired(part, "brick", 1) for part in sent[:2]]
    from_near = [paired(part, "brick", 0) for part in sent[2:]]
    halves = []
    for k, part in enumerate(from_far):
        keep, send = split_parity(k * part.shape[0], own, part, from_near[k])
        halves += [keep, swap(send, 1)]
    held = add_pair(*halves)
    image, coded = make_image(lax.all_to_all(held, ("za", "zb"), 0, 0), probes)

    held = lax.all_gather(coded, "za")
    gram = make_gram(image)
    bricks = lax.axis_size("brick")
    share = lax.all_to_all(gram.reshape(bricks, width // bricks, width), "brick", 0, 0)
    share = lax.all_to_all(spread_sum(share, n), DEPTH, 0, 0)
    parts = [held] + [swap(held, k) for k in (1, 2)]
    parts.append(swap(parts[2], 1))
    gram = lax.all_to_all(spread_sum(share, bricks), "brick", 0, 0).reshape(width, width)

    scale = math.sqrt(rows * bricks)
    upper, high, low = cholesky_and_inverse(gram, scale)
    return make_basis(parts, high, low), upper


def solution(mesh):
    deep = mesh.devices.reshape(mesh.devices.shape[0] // 4, 2, 2, mesh.devices.shape[1])
    mesh = Mesh(deep, DEPTH + ("brick",))
    in_specs = (P("brick", None), P(DEPTH, "brick", None, None, None), P(DEPTH, "brick", None))
    out_specs = (P("brick", None), P())
    return jax.shard_map(body, mesh=mesh, in_specs=in_specs, out_specs=out_specs, check_vma=False)
```
